32 devices in a mesh: dp: 4 (over x, core), seq: 4 (over z), tensor: 2 (over y).
Axes of the slice: x: 2, y: 2, z: 4, core: 2. Of those that a mesh axis runs over, the one named last changes fastest.
Arguments:
- inputs: bfloat16 [2, 4, 512, 2048], P(None, 'dp', 'seq'), may hold values from -20 to 20
- skip_mask: int32 [2, 4], P(None, 'dp'), may hold values 0 or 1
- block_order: int32 [2, 4, 8], P(None, 'dp'), may hold values from 0 to 7, as said below
- norm1_gain: bfloat16 [2048], replicated, may hold values from 0.3 to 3
- query_weight: bfloat16 [2048, 2048], P(None, 'tensor'), may hold values from -0.125 to 0.125
- key_weight: bfloat16 [2048, 1024], P(None, 'tensor'), may hold values from -0.125 to 0.125
- value_weight: bfloat16 [2048, 1024], P(None, 'tensor'), may hold values from -0.125 to 0.125
- w_out: bfloat16 [2048, 2048], P('tensor'), may hold values from -0.5 to 0.5
- norm2_gain: bfloat16 [2048], replicated, may hold values from 0.25 to 1.75
- w_gate: bfloat16 [2048, 5632], P(None, 'tensor'), may hold values from -0.125 to 0.125
- w_up: bfloat16 [2048, 5632], P(None, 'tensor'), may hold values from -0.125 to 0.125
- w_down: bfloat16 [5632, 2048], P('tensor'), may hold values from -0.078125 to 0.078125
- out_grad: bfloat16 [2, 4, 512, 2048], P(None, 'dp', 'seq'), may hold values from -6 to 6
Outputs:
- output: bfloat16 [2, 4, 512, 2048], P(None, 'dp', 'seq', 'tensor')
- input_grad: float32 [2, 4, 512, 2048], P(None, 'dp', 'seq', 'tensor')
- grad_norm1: float32 [2048], P('tensor')
- grad_query: float32 [2048, 2048], P(None, 'tensor')
- grad_key: float32 [2048, 1024], P(None, 'tensor')
- grad_value: float32 [2048, 1024], P(None, 'tensor')
- grad_out: float32 [2048, 2048], P('tensor')
- grad_norm2: float32 [2048], P('tensor')
- grad_gate: float32 [2048, 5632], P(None, 'tensor')
- grad_up: float32 [2048, 5632], P(None, 'tensor')
- grad_down: float32 [5632, 2048], P('tensor')
The draws below stay inside these ranges and needn't reach their ends.
Inputs may be any that keep to these rules, and one draw needn't show every extreme that they name: `skip_mask`: 1 marks a sample that passes through unchanged. `block_order`: each row is a permutation of the 8 position blocks in which stored blocks 2 s and 2 s + 1 hold position blocks r and 7 - r for some r, in either order, so each seq device holds one early and one late block.
All inputs are finite; a program needn't handle non-finite values. No bound on the sum of `skip_mask` on one device may be relied on, other than what follows from the above.
Results may differ from the reference program's by a relative error of at most 0.014.
The reference program's roundings to bfloat16 on the way count: a program that leaves them out, or rounds other values in their place, can miss the bound.
Values may be sent and summed in bfloat16 or wider, within the bound.
No kernel may reach another device: no remote copies, remote signals or barrier semaphores. Data moves between devices by JAX's collectives and lax.ppermute only.
A program may use at most 512 MiB of HBM per device.

```python
import jax
import jax.numpy as jnp
from jax import lax

MODEL_DIMENSION = 2048
QUERY_HEADS = 16
KEY_VALUE_HEADS = 8
HEAD_DIMENSION = 128
FF = 5632
MICRO = 2
SEQS = 4
LEN = 512
BLOCKS = 8
BLK = 64


def draw_block_order(key, part):
    samples = MICRO * SEQS
    half_count = BLOCKS // 2
    keys = jax.random.split(jax.random.fold_in(key, 11), samples)
    pairs = jax.vmap(lambda single: jax.random.permutation(single, half_count))(keys).astype(jnp.int32)
    flips = jax.random.randint(jax.random.fold_in(key, 23), (samples, half_count), 0, 2).astype(jnp.int32)
    first = jnp.where(flips == 1, BLOCKS - 1 - pairs, pairs)
    second = BLOCKS - 1 - first
    joined = jnp.stack([first, second], axis=-1).reshape(MICRO, SEQS, BLOCKS)
    return joined.astype(jnp.int32)


def draw_inputs(key, part):
    shape = (MICRO, SEQS, LEN, MODEL_DIMENSION)
    fraction = jnp.arange(MODEL_DIMENSION, dtype=jnp.float32) / (MODEL_DIMENSION - 1)
    column_scale = 0.4 * jnp.exp(fraction * jnp.log(8.0))
    noise = jnp.clip(jax.random.normal(jax.random.fold_in(key, 31), shape, jnp.float32), -6.0, 6.0)
    values = noise * column_scale
    return values.astype(jnp.bfloat16)


def draw_norm1_gain(key, part):
    fraction = jnp.arange(MODEL_DIMENSION, dtype=jnp.float32) / (MODEL_DIMENSION - 1)
    trend = 0.5 * jnp.exp(fraction * jnp.log(4.0))
    rough = 1.0 + 0.15 * jax.random.uniform(jax.random.fold_in(key, 41), (MODEL_DIMENSION,), jnp.float32, -1.0, 1.0)
    return (trend * rough).astype(jnp.bfloat16)


def place_ends(drawn, key, least, top_value):
    spot = [jax.random.randint(jax.random.fold_in(key, axis), (), 0, length) for axis, length in enumerate(drawn.shape)]
    widest = drawn.shape.index(max(drawn.shape))
    next_to = spot[:widest] + [(spot[widest] + 1) % drawn.shape[widest]] + spot[widest + 1:]
    return drawn.at[tuple(spot)].set(least).at[tuple(next_to)].set(top_value)


def steps_of(rng, dims, pieces, least, top_value):
    def one(dim, parts):
        steps = jax.random.uniform(jax.random.fold_in(jax.random.fold_in(rng, 6), dim), (parts,), jnp.float32, least / len(pieces), top_value / len(pieces))
        return jnp.repeat(jnp.exp(steps), dims[dim] // parts).reshape((-1,) + (1,) * (len(dims) - dim - 1))

    level = one(*pieces[0])
    for cut in pieces[1:]:
        level = level * one(*cut)
    return level


def centred(own_key, dims, deviation, limit, shards=(), kind=jnp.bfloat16):
    factor_of = steps_of(own_key, dims, shards, -0.22, 0.18) if shards else 1.0
    values = jax.random.normal(own_key, dims, jnp.float32) * deviation * factor_of
    return jnp.minimum(jnp.maximum(values, -limit), limit).astype(kind)


def setup_inputs(seed: int = 0) -> dict:
    streams_of = jax.random.split(jax.random.key(seed), 14)
    inputs = draw_inputs(jax.random.fold_in(streams_of[13], 71), 0)
    skip_mask = place_ends((jax.random.randint(streams_of[1], (MICRO, SEQS), 0, 3) < 1).astype(jnp.int32), jax.random.fold_in(streams_of[1], 1), 0, 1)
    block_order = draw_block_order(jax.random.fold_in(streams_of[13], 71), 0)
    norm1_gain = draw_norm1_gain(jax.random.fold_in(streams_of[13], 71), 0)
    query_weight = centred(streams_of[4], (MODEL_DIMENSION, QUERY_HEADS * HEAD_DIMENSION), MODEL_DIMENSION ** -0.5, 0.125, ((1, 2),))
    key_weight = centred(streams_of[5], (MODEL_DIMENSION, KEY_VALUE_HEADS * HEAD_DIMENSION), MODEL_DIMENSION ** -0.5, 0.125, ((1, 2),))
    value_weight = centred(streams_of[6], (MODEL_DIMENSION, KEY_VALUE_HEADS * HEAD_DIMENSION), MODEL_DIMENSION ** -0.5, 0.125, ((1, 2),))
    w_out = centred(streams_of[7], (QUERY_HEADS * HEAD_DIMENSION, MODEL_DIMENSION), (QUERY_HEADS * HEAD_DIMENSION // 16) ** -0.5, 0.5, ((0, 2),))
    norm2_gain = jnp.clip(1.0 + 0.15 * jax.random.normal(streams_of[8], (MODEL_DIMENSION,), jnp.float32), 0.25, 1.75).astype(jnp.bfloat16)
    w_gate = centred(streams_of[9], (MODEL_DIMENSION, FF), MODEL_DIMENSION ** -0.5, 0.125, ((1, 2),))
    w_up = centred(streams_of[10], (MODEL_DIMENSION, FF), MODEL_DIMENSION ** -0.5, 0.125, ((1, 2),))
    w_down = centred(streams_of[11], (FF, MODEL_DIMENSION), FF ** -0.5, 0.078125, ((0, 2),))
    out_grad = centred(streams_of[12], (MICRO, SEQS, LEN, MODEL_DIMENSION), 1.0, 6.0, ((1, 4), (2, 4)))
    return dict(inputs=inputs, skip_mask=skip_mask, block_order=block_order, norm1_gain=norm1_gain, query_weight=query_weight, key_weight=key_weight, value_weight=value_weight, w_out=w_out, norm2_gain=norm2_gain, w_gate=w_gate, w_up=w_up, w_down=w_down, out_grad=out_grad)


EPSILON = 1e-05
NEGATIVE = -1e+30
PRECISE = lax.Precision.HIGHEST

@jax.custom_vjp
def lower_bound(v):
    return lax.optimization_barrier(v.astype(jnp.bfloat16)).astype(jnp.float32)

@jax.custom_vjp
def lower_bound_backward(v):
    return v

def low_keep(v):
    return (lower_bound(v), None)

def low_pass(kept, grad):
    return (grad,)

def back_keep(v):
    return (v, None)

def back_low(kept, grad):
    return (lower_bound(grad),)
lower_bound.defvjp(low_keep, low_pass)
lower_bound_backward.defvjp(back_keep, back_low)

def matrix_product(left, right):
    return jnp.dot(left, right, precision=PRECISE)

def angles(positions, head_width):
    frequency = jnp.exp(jnp.arange(head_width // 2, dtype=jnp.float32) * (-2.0 / head_width) * jnp.log(10000.0))
    phases = positions.astype(jnp.float32)[:, None] * frequency[None, :]
    return (jnp.cos(phases), jnp.sin(phases))

def rotate(values, cos_table, sine_table):
    half_width = values.shape[-1] // 2
    lower_half = values[..., :half_width]
    upper_half = values[..., half_width:]
    return jnp.concatenate([lower_half * cos_table - upper_half * sine_table, upper_half * cos_table + lower_half * sine_table], axis=-1)

def decoder_layer(inputs_f, gain_one, query_weight, key_weight, value_weight, w_out, gain_two, w_gate, w_up, w_down, positions, active):
    token_length = inputs_f.shape[0]
    group_total = QUERY_HEADS // KEY_VALUE_HEADS
    scale_one = lax.rsqrt(lax.optimization_barrier(jnp.mean(inputs_f * inputs_f, axis=-1, keepdims=True)) + EPSILON)
    first_normalized = lower_bound(inputs_f * scale_one * gain_one)
    cos_table, sine_table = angles(positions, HEAD_DIMENSION)
    query_unrotated = lower_bound_backward(matrix_product(first_normalized, query_weight)).reshape(token_length, KEY_VALUE_HEADS, group_total, HEAD_DIMENSION)
    key_unrotated = lower_bound_backward(matrix_product(first_normalized, key_weight)).reshape(token_length, KEY_VALUE_HEADS, HEAD_DIMENSION)
    value_matrix_rows = lower_bound_backward(lower_bound(matrix_product(first_normalized, value_weight))).reshape(token_length, KEY_VALUE_HEADS, HEAD_DIMENSION)
    queries = lower_bound(rotate(query_unrotated, cos_table[:, None, None, :], sine_table[:, None, None, :]))
    key_rows = lower_bound(rotate(key_unrotated, cos_table[:, None, :], sine_table[:, None, :]))
    raw_scores = lower_bound_backward(jnp.einsum('rkgd,lkd->kgrl', queries, key_rows, precision=PRECISE))
    allowed = positions[None, :] <= positions[:, None]
    scores = jnp.where(allowed[None, None], raw_scores * HEAD_DIMENSION ** (-0.5), NEGATIVE)
    attn_weights = jax.nn.softmax(scores, axis=-1)
    attended = jnp.einsum('kgrl,lkd->rkgd', lower_bound(attn_weights), value_matrix_rows, precision=PRECISE).reshape(token_length, QUERY_HEADS * HEAD_DIMENSION)
    attended = lower_bound_backward(lower_bound(attended))
    mixed_out = lower_bound_backward(matrix_product(attended, w_out))
    hidden = inputs_f + active * mixed_out
    scale_two = lax.rsqrt(lax.optimization_barrier(jnp.mean(hidden * hidden, axis=-1, keepdims=True)) + EPSILON)
    normed_two = lower_bound(hidden * scale_two * gain_two)
    gate_rows = lower_bound_backward(matrix_product(normed_two, w_gate))
    up_rows = lower_bound_backward(matrix_product(normed_two, w_up))
    gated = lower_bound(jax.nn.silu(gate_rows) * up_rows)
    branch = lower_bound_backward(matrix_product(gated, w_down))
    return hidden + active * branch

def reference(inputs, skip_mask, block_order, norm1_gain, query_weight, key_weight, value_weight, w_out, norm2_gain, w_gate, w_up, w_down, out_grad):
    params = tuple((element.astype(jnp.float32) for element in (norm1_gain, query_weight, key_weight, value_weight, w_out, norm2_gain, w_gate, w_up, w_down)))
    samples = MICRO * SEQS
    flat_in = inputs.reshape(samples, LEN, MODEL_DIMENSION)
    flat_grad = out_grad.reshape(samples, LEN, MODEL_DIMENSION)
    flat_skip = skip_mask.reshape(samples)
    flat_order = block_order.reshape(samples, BLOCKS)

    def one_sample(totals, packed):
        sample_in, sample_grad, sample_skip, sample_order = packed
        positions = (sample_order[:, None] * BLK + jnp.arange(BLK, dtype=jnp.int32)[None, :]).reshape(LEN)
        active = (1 - sample_skip).astype(jnp.float32)

        def forward(inputs_f, *weights):
            return decoder_layer(inputs_f, *weights, positions, active)
        result, pullback = jax.vjp(forward, sample_in.astype(jnp.float32), *params)
        gradients = pullback(sample_grad.astype(jnp.float32))
        totals = jax.tree.map(lambda former, latter: former + latter, totals, tuple(gradients[1:]))
        return (totals, (result.astype(jnp.bfloat16), gradients[0]))
    starts = tuple((jnp.zeros_like(element) for element in params))
    totals, (results, in_grads) = lax.scan(one_sample, starts, (flat_in, flat_grad, flat_skip, flat_order))
    return (results.reshape(MICRO, SEQS, LEN, MODEL_DIMENSION), in_grads.reshape(MICRO, SEQS, LEN, MODEL_DIMENSION), totals[0], totals[1], totals[2], totals[3], totals[4], totals[5], totals[6], totals[7], totals[8])
```

```python
import jax
import jax.numpy as jnp
from jax import lax
from jax.sharding import PartitionSpec as P

HEAD_DIMENSION = 128
EPSILON = 1e-05
NEGATIVE = -1e30
BF = jnp.bfloat16
F32 = jnp.float32


def angles(positions, head_width):
    frequency = jnp.exp(
        jnp.arange(head_width // 2, dtype=F32) * (-2.0 / head_width) * jnp.log(10000.0)
    )
    phases = positions.astype(F32)[:, None] * frequency[None, :]
    return (jnp.cos(phases), jnp.sin(phases))


def rotate(values, cos_table, sine_table, direction):
    half_width = values.shape[-1] // 2
    lower_half = values[..., :half_width]
    upper_half = values[..., half_width:]
    return jnp.concatenate(
        [
            lower_half * cos_table - direction * upper_half * sine_table,
            upper_half * cos_table + direction * lower_half * sine_table,
        ],
        axis=-1,
    )


def dot(a, b):
    return jnp.dot(a, b, preferred_element_type=F32)


def dot_t(a, b):
    return lax.dot_general(a, b, (((1,), (1,)), ((), ())), preferred_element_type=F32)


def dot_rows(a, b):
    return lax.dot_general(a, b, (((0,), (0,)), ((), ())), preferred_element_type=F32)


def sum_tensor(part):
    sent = part.astype(BF)
    if lax.axis_size("tensor") == 2:
        other = lax.ppermute(sent, "tensor", [(0, 1), (1, 0)])
        return sent.astype(F32) + other.astype(F32)
    return lax.psum(sent.astype(F32), "tensor")


def half(values, index):
    width = values.shape[1] // 2
    return lax.dynamic_slice_in_dim(values, index * width, width, 1)


def spread(by_core, by_chip):
    count = lax.axis_size("dp")
    me = lax.axis_index("dp")
    blocks = []
    for mask in range(count):
        target = jnp.bitwise_xor(me, mask)
        block = jnp.concatenate(
            [half(v, target % 2) for v in by_core] + [half(v, target // 2) for v in by_chip], axis=1
        )
        if mask:
            block = lax.ppermute(block, "dp", [(i, i ^ mask) for i in range(count)])
        blocks.append(block)
    return jnp.concatenate(blocks, axis=0)


def finish(quarter, row_by_core):
    part = lax.psum_scatter(quarter.astype(BF), "seq", scatter_dimension=0, tiled=True)
    every = lax.all_gather(part, ("dp", "seq"), axis=0, tiled=False)
    seq = lax.axis_size("seq")
    every = every.reshape(2, 2, seq, part.shape[0], part.shape[1])
    return every, row_by_core


def assemble(every, row_by_core, start, stop):
    every = every[..., start:stop]
    order = (1, 2, 3, 0, 4) if row_by_core else (0, 2, 3, 1, 4)
    _, _, seq, rows, cols = every.shape
    return every.transpose(order).reshape(2 * seq * rows, 2 * cols).astype(F32)


def on_device(
    inputs,
    skip_mask,
    block_order,
    norm1_gain,
    query_weight,
    key_weight,
    value_weight,
    w_out,
    norm2_gain,
    w_gate,
    w_up,
    w_down,
    out_grad,
):
    tensor_count = lax.axis_size("tensor")
    tensor_rank = lax.axis_index("tensor")
    seq_rank = lax.axis_index("seq")
    micro, _, length, width = inputs.shape
    rows = micro * length
    slice_width = width // tensor_count
    kv = key_weight.shape[1] // HEAD_DIMENSION
    group = query_weight.shape[1] // key_weight.shape[1]
    block_rows = length // 2
    col_start = tensor_rank * slice_width

    def mine(values):
        return lax.dynamic_slice_in_dim(values, col_start, slice_width, values.ndim - 1)

    gain_one = norm1_gain.astype(F32)
    gain_two = norm2_gain.astype(F32)
    gain_one_s = mine(gain_one)

    in_f = inputs.reshape(rows, width).astype(F32)
    grad_f = out_grad.reshape(rows, width).astype(F32)
    active = jnp.repeat((1 - skip_mask[:, 0]).astype(F32), length)[:, None]
    offsets = jnp.arange(block_rows, dtype=jnp.int32)
    order = block_order[:, 0]
    all_pos = (order[:, :, None] * block_rows + offsets).reshape(micro, -1)
    my_blocks = lax.dynamic_slice_in_dim(order, 2 * seq_rank, 2, 1)
    local_pos = (my_blocks[:, :, None] * block_rows + offsets).reshape(micro, length)
    cos_table, sine_table = angles(local_pos.reshape(-1), HEAD_DIMENSION)
    cos_table, sine_table = cos_table[:, None, :], sine_table[:, None, :]
    allowed = all_pos[:, None, :] <= local_pos[:, :, None]

    scale_one = lax.rsqrt(jnp.mean(in_f * in_f, axis=-1, keepdims=True) + EPSILON)
    hn1 = (in_f * scale_one * gain_one).astype(BF)
    df = (active * grad_f).astype(BF)
    early = spread([hn1, df], [])

    q = rotate(dot(hn1, query_weight).reshape(rows, -1, HEAD_DIMENSION), cos_table, sine_table, 1.0)
    k = rotate(dot(hn1, key_weight).reshape(rows, -1, HEAD_DIMENSION), cos_table, sine_table, 1.0)
    v = dot(hn1, value_weight).astype(BF)
    q = q.astype(BF).reshape(micro, length, kv, group, HEAD_DIMENSION)
    kvb = jnp.concatenate([k.astype(BF).reshape(rows, -1), v], axis=1).reshape(micro, length, -1)
    kv_all = [lax.all_gather(kvb[m], "seq", axis=0, tiled=True) for m in range(micro)]
    k_all = [a[:, : kv * HEAD_DIMENSION].reshape(-1, kv, HEAD_DIMENSION) for a in kv_all]
    v_all = [a[:, kv * HEAD_DIMENSION :].reshape(-1, kv, HEAD_DIMENSION) for a in kv_all]

    dz = dot_t(df, w_down)

    probs = []
    mixed = []
    attended = []
    for m in range(micro):
        raw = jnp.einsum("rkgd,lkd->kgrl", q[m], k_all[m], preferred_element_type=F32)
        scores = jnp.where(allowed[m][None, None], raw * HEAD_DIMENSION ** (-0.5), NEGATIVE)
        top = jnp.max(scores, axis=-1, keepdims=True)
        expd = jnp.exp(scores - top)
        prob = expd / jnp.sum(expd, axis=-1, keepdims=True)
        probs.append(prob)
        o = jnp.einsum("kgrl,lkd->rkgd", prob.astype(BF), v_all[m], preferred_element_type=F32)
        o = o.reshape(length, -1).astype(BF)
        attended.append(o)
        mixed.append(sum_tensor(dot(o, w_out)))
    mixed = jnp.concatenate(mixed, axis=0)
    ob = jnp.concatenate(attended, axis=0)

    hidden = in_f + active * mixed
    scale_two = lax.rsqrt(jnp.mean(hidden * hidden, axis=-1, keepdims=True) + EPSILON)
    hn2 = (hidden * scale_two * gain_two).astype(BF)
    g = dot(hn2, w_gate)
    u = dot(hn2, w_up)
    sig = jax.nn.sigmoid(g)
    silu = g * sig
    z = (silu * u).astype(BF)
    dg = (dz * u * sig * (1.0 + g * (1.0 - sig))).astype(BF)
    du = (dz * silu).astype(BF)
    ffn_half = z.shape[1] // 2
    core_half = width // 2

    middle = spread([hn2], [z])
    late = spread([], [dg, du])
    down_q = dot_rows(middle[:, core_half:], early[:, core_half:])
    down_all = finish(down_q, False)
    gate_up_q = dot_rows(middle[:, :core_half], late)
    gate_up_all = finish(gate_up_q, True)

    dn2 = sum_tensor(dot_t(dg, w_gate) + dot_t(du, w_up))
    branch = lax.psum_scatter(
        dot(z, w_down).astype(BF), "tensor", scatter_dimension=1, tiled=True
    ).astype(F32)
    output = (mine(hidden) + active * branch).astype(BF)

    d_scaled = dn2 * gain_two
    inner_two = jnp.mean(d_scaled * hidden, axis=-1, keepdims=True)
    dh = grad_f + scale_two * d_scaled - hidden * scale_two**3 * inner_two
    gain_terms = mine(jnp.sum(dn2 * hidden * scale_two, axis=0))
    da = (active * dh).astype(BF)
    do = dot_t(da, w_out).astype(BF).reshape(micro, length, kv, group, HEAD_DIMENSION)
    out_act = spread([da], [ob])
    out_q = dot_rows(out_act[:, core_half:], out_act[:, :core_half])
    out_all = finish(out_q, False)

    dqs = []
    dkvs = []
    for m in range(micro):
        prob = probs[m]
        dp = jnp.einsum("rkgd,lkd->kgrl", do[m], v_all[m], preferred_element_type=F32)
        inner = jnp.sum(prob * dp, axis=-1, keepdims=True)
        ds = (prob * (dp - inner) * HEAD_DIMENSION ** (-0.5)).astype(BF)
        dqs.append(jnp.einsum("kgrl,lkd->rkgd", ds, k_all[m], preferred_element_type=F32))
        dk = jnp.einsum("kgrl,rkgd->lkd", ds, q[m], preferred_element_type=F32)
        dv = jnp.einsum("kgrl,rkgd->lkd", prob.astype(BF), do[m], preferred_element_type=F32)
        dkv = jnp.concatenate([dk.reshape(dk.shape[0], -1), dv.reshape(dv.shape[0], -1)], axis=1)
        dkvs.append(lax.psum_scatter(dkv.astype(BF), "seq", scatter_dimension=0, tiled=True))
    dq = jnp.stack(dqs).reshape(rows, -1, HEAD_DIMENSION)
    dkv = jnp.stack(dkvs).reshape(rows, -1).astype(F32)
    dk = dkv[:, : kv * HEAD_DIMENSION].reshape(rows, -1, HEAD_DIMENSION)
    dqb = rotate(dq, cos_table, sine_table, -1.0).reshape(rows, -1).astype(BF)
    dkb = rotate(dk, cos_table, sine_table, -1.0).reshape(rows, -1).astype(BF)
    dvb = dkv[:, kv * HEAD_DIMENSION :].astype(BF)

    qkv_act = spread([], [dqb, dkb, dvb])
    qkv_q = dot_rows(early[:, :core_half], qkv_act)
    qkv_all = finish(qkv_q, True)

    dn1 = dot_t(dqb, query_weight) + dot_t(dkb, key_weight) + dot_t(dvb, value_weight)
    dn1 = lax.psum_scatter(dn1, "tensor", scatter_dimension=1, tiled=True)
    d_scaled_one = dn1 * gain_one_s
    in_slice = mine(in_f)
    inner_one = lax.psum(jnp.sum(d_scaled_one * in_slice, axis=-1, keepdims=True), "tensor")
    input_grad = (
        mine(dh) + scale_one * d_scaled_one - in_slice * scale_one**3 * (inner_one / width)
    )
    gains = jnp.stack([jnp.sum(dn1 * in_slice * scale_one, axis=0), gain_terms])
    gains = lax.psum(gains, ("dp", "seq"))

    q_half = dqb.shape[1] // 2
    k_half = dkb.shape[1] // 2
    return (
        output.reshape(micro, 1, length, slice_width),
        input_grad.reshape(micro, 1, length, slice_width),
        gains[0],
        assemble(*qkv_all, 0, q_half),
        assemble(*qkv_all, q_half, q_half + k_half),
        assemble(*qkv_all, q_half + k_half, q_half + 2 * k_half),
        assemble(*out_all, 0, core_half),
        gains[1],
        assemble(*gate_up_all, 0, ffn_half),
        assemble(*gate_up_all, ffn_half, 2 * ffn_half),
        assemble(*down_all, 0, core_half),
    )


def solution(mesh):
    return jax.shard_map(
        on_device,
        mesh=mesh,
        in_specs=(
            P(None, "dp", "seq", None),
            P(None, "dp"),
            P(None, "dp", None),
            P(),
            P(None, "tensor"),
            P(None, "tensor"),
            P(None, "tensor"),
            P("tensor", None),
            P(),
            P(None, "tensor"),
            P(None, "tensor"),
            P("tensor", None),
            P(None, "dp", "seq", None),
        ),
        out_specs=(
            P(None, "dp", "seq", "tensor"),
            P(None, "dp", "seq", "tensor"),
            P("tensor"),
            P(None, "tensor"),
            P(None, "tensor"),
            P(None, "tensor"),
            P("tensor", None),
            P("tensor"),
            P(None, "tensor"),
            P(None, "tensor"),
            P("tensor", None),
        ),
        check_vma=False,
    )
```

```python
import functools

import jax
import jax.numpy as jnp
from jax import lax
from jax.experimental import pallas as pl
from jax.experimental.pallas import tpu as pltpu
from jax.sharding import PartitionSpec as P

HEAD_DIMENSION = 128
EPSILON = 1e-05
NEGATIVE = -1e30
BF = jnp.bfloat16
F32 = jnp.float32
ACROSS = [(0, 2), (2, 0), (1, 3), (3, 1)]
CORES = [(0, 1), (1, 0), (2, 3), (3, 2)]
PAIRS = [(0, 1), (1, 0), (2, 3), (3, 2)]
MIDDLE = [(1, 2), (2, 1)]
QKV_CHUNKS = 2


def dot(a, b):
    return jnp.dot(a, b, preferred_element_type=F32)


def dot_t(a, b):
    return lax.dot_general(a, b, (((1,), (1,)), ((), ())), preferred_element_type=F32)


def dot_rows(a, b):
    out = lax.dot_general(a, b, (((0,), (0,)), ((), ())), preferred_element_type=F32)
    return out.astype(BF)


def swap_tensor(sent):
    if lax.axis_size("tensor") == 2:
        return lax.ppermute(sent, "tensor", [(0, 1), (1, 0)]).astype(F32)
    return lax.psum(sent.astype(F32), "tensor") - sent.astype(F32)


def half(values, index):
    width = values.shape[1] // 2
    return lax.dynamic_slice_in_dim(values, index * width, width, 1)


def to_core(sent):
    return lax.ppermute(sent, "dp", CORES)


def to_chip(sent):
    return lax.ppermute(sent, "dp", ACROSS)


def fits(rows, widths):
    return rows % 16 == 0 and all(w % 128 == 0 for w in widths)


def tables(positions):
    half_width = HEAD_DIMENSION // 2
    frequency = jnp.exp(
        jnp.arange(half_width, dtype=F32) * (-2.0 / HEAD_DIMENSION) * jnp.log(10000.0)
    )
    phases = positions.astype(F32)[:, None] * frequency[None, :]
    cos, sin = jnp.cos(phases), jnp.sin(phases)
    return jnp.concatenate([cos, cos], axis=1), jnp.concatenate([-sin, sin], axis=1)


def turn(values, cos, sin):
    return values * cos + pltpu.roll(values, HEAD_DIMENSION // 2, 1) * sin


def key_value_kernel(x_ref, key_ref, value_ref, cos_ref, sin_ref, out_ref):
    x = x_ref[...]
    keys = turn(dot(x, key_ref[...]), cos_ref[...], sin_ref[...])
    out_ref[:, :HEAD_DIMENSION] = keys.astype(BF)
    out_ref[:, HEAD_DIMENSION:] = dot(x, value_ref[...]).astype(BF)


def keys_and_values(x, key_weight, value_weight, cos, sin):
    rows, width = x.shape
    heads = key_weight.shape[1] // HEAD_DIMENSION
    whole = lambda step: (0, 0)
    column = lambda step: (0, step)
    return pl.pallas_call(
        key_value_kernel,
        grid=(heads,),
        in_specs=[
            pl.BlockSpec((rows, width), whole),
            pl.BlockSpec((width, HEAD_DIMENSION), column),
            pl.BlockSpec((width, HEAD_DIMENSION), column),
            pl.BlockSpec((rows, HEAD_DIMENSION), whole),
            pl.BlockSpec((rows, HEAD_DIMENSION), whole),
        ],
        out_specs=pl.BlockSpec((rows, 2 * HEAD_DIMENSION), column),
        out_shape=jax.ShapeDtypeStruct((rows, 2 * heads * HEAD_DIMENSION), BF),
        name="keys_and_values",
    )(x, key_weight, value_weight, cos, sin)


def query_kernel(x_ref, weight_ref, cos_ref, sin_ref, out_ref):
    raw = dot(x_ref[...], weight_ref[...])
    for start in range(0, raw.shape[1], HEAD_DIMENSION):
        head = raw[:, start : start + HEAD_DIMENSION]
        turned = turn(head, cos_ref[...], sin_ref[...])
        out_ref[:, start : start + HEAD_DIMENSION] = turned.astype(BF)


def queries(x, weight, cos, sin):
    rows, width = x.shape
    block = 2 * HEAD_DIMENSION
    whole = lambda step: (0, 0)
    column = lambda step: (0, step)
    return pl.pallas_call(
        query_kernel,
        grid=(weight.shape[1] // block,),
        in_specs=[
            pl.BlockSpec((rows, width), whole),
            pl.BlockSpec((width, block), column),
            pl.BlockSpec((rows, HEAD_DIMENSION), whole),
            pl.BlockSpec((rows, HEAD_DIMENSION), whole),
        ],
        out_specs=pl.BlockSpec((rows, block), column),
        out_shape=jax.ShapeDtypeStruct((rows, weight.shape[1]), BF),
        cost_estimate=pl.CostEstimate(
            flops=2 * rows * width * weight.shape[1],
            bytes_accessed=2 * width * weight.shape[1] + 2 * rows * width,
            transcendentals=0,
        ),
        name="queries",
    )(x, weight, cos, sin)


def probabilities(query, keys, query_pos, key_pos):
    scores = dot_t(query, keys) * HEAD_DIMENSION ** (-0.5)
    scores = jnp.where(key_pos <= query_pos, scores, NEGATIVE)
    expd = jnp.exp(scores - jnp.max(scores, axis=-1, keepdims=True))
    return expd / jnp.sum(expd, axis=-1, keepdims=True)


def attend_kernel(q_ref, kv_ref, query_pos_ref, key_pos_ref, out_ref):
    keys = kv_ref[:, :HEAD_DIMENSION]
    values = kv_ref[:, HEAD_DIMENSION:]
    for start in range(0, q_ref.shape[1], HEAD_DIMENSION):
        head = slice(start, start + HEAD_DIMENSION)
        prob = probabilities(q_ref[:, head], keys, query_pos_ref[...], key_pos_ref[...])
        out_ref[:, head] = dot(prob.astype(BF), values).astype(BF)


def attend_back_kernel(
    q_ref, kv_ref, query_pos_ref, key_pos_ref, do_ref, cos_ref, sin_ref, dq_ref, dkv_ref
):
    keys = kv_ref[:, :HEAD_DIMENSION]
    values = kv_ref[:, HEAD_DIMENSION:]
    dk = dv = None
    for start in range(0, q_ref.shape[1], HEAD_DIMENSION):
        head = slice(start, start + HEAD_DIMENSION)
        query = q_ref[:, head]
        do = do_ref[:, head]
        prob = probabilities(query, keys, query_pos_ref[...], key_pos_ref[...])
        dp = dot_t(do, values)
        inner = jnp.sum(prob * dp, axis=-1, keepdims=True)
        ds = (prob * (dp - inner) * HEAD_DIMENSION ** (-0.5)).astype(BF)
        dq = dot(ds, keys)
        dq_ref[:, head] = turn(dq, cos_ref[...], -sin_ref[...]).astype(BF)
        part_k = lax.dot_general(ds, query, (((0,), (0,)), ((), ())), preferred_element_type=F32)
        part_v = lax.dot_general(
            prob.astype(BF), do, (((0,), (0,)), ((), ())), preferred_element_type=F32
        )
        dk = part_k if dk is None else dk + part_k
        dv = part_v if dv is None else dv + part_v
    dkv_ref[:, :HEAD_DIMENSION] = dk.astype(BF)
    dkv_ref[:, HEAD_DIMENSION:] = dv.astype(BF)


def attention(m, length, q, kv_all, query_pos, key_pos, do=None, cos=None, sin=None):
    total = kv_all.shape[0]
    heads = kv_all.shape[1] // (2 * HEAD_DIMENSION)
    block = q.shape[1] // heads
    in_rows = lambda h: (m, h)
    column = lambda h: (0, h)
    in_specs = [
        pl.BlockSpec((length, block), in_rows),
        pl.BlockSpec((total, 2 * HEAD_DIMENSION), column),
        pl.BlockSpec((length, 1), lambda h: (m, 0)),
        pl.BlockSpec((None, 1, total), lambda h: (m, 0, 0)),
    ]
    operands = [q, kv_all, query_pos, key_pos]
    out_specs = pl.BlockSpec((length, block), column)
    out_shape = jax.ShapeDtypeStruct((length, q.shape[1]), BF)
    kernel = attend_kernel
    if do is not None:
        kernel = attend_back_kernel
        in_specs += [pl.BlockSpec((length, block), in_rows)]
        in_specs += [pl.BlockSpec((length, HEAD_DIMENSION), lambda h: (m, 0))] * 2
        operands += [do, cos, sin]
        out_specs = [out_specs, pl.BlockSpec((total, 2 * HEAD_DIMENSION), column)]
        out_shape = [out_shape, jax.ShapeDtypeStruct(kv_all.shape, BF)]
    return pl.pallas_call(
        kernel,
        grid=(heads,),
        in_specs=in_specs,
        out_specs=out_specs,
        out_shape=out_shape,
        cost_estimate=pl.CostEstimate(
            flops=(4 if do is None else 10) * length * total * q.shape[1],
            bytes_accessed=8 * kv_all.size,
            transcendentals=length * total * q.shape[1] // HEAD_DIMENSION,
        ),
        name="attend" if do is None else "attend_back",
    )(*operands)


def turn_back_kernel(dkv_ref, cos_ref, sin_ref, dk_ref, dv_ref):
    dk = dkv_ref[:, :HEAD_DIMENSION].astype(F32)
    dk_ref[...] = turn(dk, cos_ref[...], -sin_ref[...]).astype(BF)
    dv_ref[...] = dkv_ref[:, HEAD_DIMENSION:]


def turn_back(dkv, cos, sin):
    rows, both = dkv.shape
    column = lambda h: (0, h)
    return pl.pallas_call(
        turn_back_kernel,
        grid=(both // (2 * HEAD_DIMENSION),),
        in_specs=[pl.BlockSpec((rows, 2 * HEAD_DIMENSION), column)]
        + [pl.BlockSpec((rows, HEAD_DIMENSION), lambda h: (0, 0))] * 2,
        out_specs=[pl.BlockSpec((rows, HEAD_DIMENSION), column)] * 2,
        out_shape=[jax.ShapeDtypeStruct((rows, both // 2), BF)] * 2,
        name="turn_back",
    )(dkv, cos, sin)


def place_kernel(index_ref, *refs, widths, split):
    outs = refs[len(refs) - len(widths) :]
    step = pl.program_id(0)
    for number in range(4):

        @pl.when(step // split == number)
        def _(source=refs[number]):
            start = 0
            for width, out in zip(widths, outs):
                out[...] = source[:, start : start + width].astype(F32)
                start += width


def place(previous, pieces, row, quarter_rows, widths, row_by_core):
    rows, cols = pieces[0].shape
    me = lax.axis_index("dp")
    if not fits(rows, widths):
        outs = []
        start = 0
        for number, width in enumerate(widths):
            buffer = jnp.zeros((2 * quarter_rows, 2 * width), F32)
            if previous is not None:
                buffer = previous[number]
            for piece, mask in zip(pieces, (0, 2, 1, 3)):
                other = jnp.bitwise_xor(me, mask)
                chip, core = other // 2, other % 2
                first, second = (core, chip) if row_by_core else (chip, core)
                at = (first * quarter_rows + row, second * width)
                source = piece[:, start : start + width].astype(F32)
                buffer = lax.dynamic_update_slice(buffer, source, at)
            outs.append(buffer)
            start += width
        return outs
    split = 2 if rows % 32 == 0 else 1
    part = rows // split

    def out_index(step, index_ref):
        piece = step // split
        chip = jnp.where(piece % 2 == 0, index_ref[0], 1 - index_ref[0])
        core = jnp.where(piece < 2, index_ref[1], 1 - index_ref[1])
        first, second = (core, chip) if row_by_core else (chip, core)
        return first * (quarter_rows // part) + row // part + step % split, second

    def in_index(number):
        return lambda step, _: (jnp.clip(step - number * split, 0, split - 1), 0)

    in_specs = [pl.BlockSpec((part, cols), in_index(n)) for n in range(4)]
    operands = [jnp.stack([me // 2, me % 2]).astype(jnp.int32)] + list(pieces)
    aliases = {}
    if previous is not None:
        for number, buffer in enumerate(previous):
            in_specs.append(pl.BlockSpec(memory_space=pl.ANY))
            aliases[len(operands)] = number
            operands.append(buffer)
    return pl.pallas_call(
        functools.partial(place_kernel, widths=widths, split=split),
        grid_spec=pltpu.PrefetchScalarGridSpec(
            num_scalar_prefetch=1,
            grid=(4 * split,),
            in_specs=in_specs,
            out_specs=[pl.BlockSpec((part, width), out_index) for width in widths],
        ),
        out_shape=[jax.ShapeDtypeStruct((2 * quarter_rows, 2 * w), F32) for w in widths],
        input_output_aliases=aliases,
        cost_estimate=pl.CostEstimate(
            flops=0, bytes_accessed=24 * rows * cols, transcendentals=0
        ),
        name="place",
    )(*operands)


def share_kernel(every_ref, *out_refs, pieces):
    out_refs = list(out_refs)
    for start, stop, widths in pieces:
        at = 0
        for width in widths:
            out_refs.pop(0)[...] = every_ref[start:stop, at : at + width].astype(F32)
            at += width


def write_whole(every, pieces):
    count, rows, cols = every.shape
    seq = lax.axis_size("seq")
    aligned = all(size % 16 == 0 and all(w % 128 == 0 for w in ws) for size, ws, _ in pieces)
    if not aligned:
        results = []
        start = 0
        for size, widths, row_by_core in pieces:
            at = 0
            for width in widths:
                piece = every[:, start : start + size, at : at + width]
                piece = piece.reshape(2, 2, seq, size, width)
                piece = piece.transpose((1, 2, 3, 0, 4) if row_by_core else (0, 2, 3, 1, 4))
                results.append(piece.reshape(2 * seq * size, 2 * width).astype(F32))
                at += width
            start += size
        return results
    spans = []
    out_specs = []
    out_shape = []
    start = 0
    for size, widths, row_by_core in pieces:
        spans.append((start, start + size, widths))

        def index(device, row_by_core=row_by_core):
            chip, core, rank = device // (2 * seq), (device // seq) % 2, device % seq
            row, column = (core, chip) if row_by_core else (chip, core)
            return row * seq + rank, column

        for width in widths:
            out_specs.append(pl.BlockSpec((size, width), index))
            out_shape.append(jax.ShapeDtypeStruct((2 * seq * size, 2 * width), F32))
        start += size
    return pl.pallas_call(
        functools.partial(share_kernel, pieces=tuple(spans)),
        grid=(count,),
        in_specs=[pl.BlockSpec((None, rows, cols), lambda device: (device, 0, 0))],
        out_specs=out_specs,
        out_shape=out_shape,
        cost_estimate=pl.CostEstimate(
            flops=0, bytes_accessed=6 * every.size, transcendentals=0
        ),
        name="write_whole",
    )(every)


class Chain:
    def __init__(self):
        rank = lax.axis_index("seq")
        self.is_middle = (rank == 1) | (rank == 2)
        self.stages = {n: [] for n in ("in", "middle", "out", "across", "core")}
        self.outs = {}
        self.time = 0
        self.fresh = []
        self.writes = []
        self.arrived = []

    def add(self, name, quarter, count, widths, row_by_core):
        size = quarter.shape[0] // count
        for i in range(count):
            info = (name, i * size, quarter.shape[0], widths, row_by_core)
            self.stages["in"].append((0, quarter[i * size : (i + 1) * size], info))

    def busy(self):
        return bool(self.writes) or any(self.stages.values())

    def put(self, stage, value, info):
        self.stages[stage].append((self.time + 1, value, info))

    def tick(self, *values):
        self.time += 1
        taken = {}
        for name, queue in self.stages.items():
            if queue and queue[0][0] <= self.time:
                taken[name] = queue.pop(0)
        names = list(taken)
        done = self.arrived
        writes, self.writes = self.writes, []
        fresh, self.fresh = self.fresh, []
        flat = [taken[n][1] for n in names]
        flat += [a for pieces, _ in writes for a in pieces]
        flat += [b for n in fresh for b in self.outs[n]]
        tied = list(lax.optimization_barrier(tuple(flat) + tuple(done) + tuple(values)))
        values = tied[len(tied) - len(values) :] if values else []
        now = {n: tied.pop(0) for n in names}
        writes = [([tied.pop(0) for _ in pieces], info) for pieces, info in writes]
        for n in fresh:
            self.outs[n] = [tied.pop(0) for _ in self.outs[n]]
        meta = {n: taken[n][2] for n in names}
        arrived = []
        if "middle" in now:
            other = lax.ppermute(now["middle"], "seq", MIDDLE)
            arrived.append(other)
            self.put("out", now["middle"] + other, meta["middle"])
        if "in" in now:
            other = lax.ppermute(now["in"], "seq", [(0, 1), (3, 2)])
            arrived.append(other)
            self.put("middle", now["in"] + other, meta["in"])
        if "out" in now:
            other = lax.ppermute(now["out"], "seq", [(1, 0), (2, 3)])
            arrived.append(other)
            self.put("across", jnp.where(self.is_middle, now["out"], other), meta["out"])
        if "across" in now:
            other = to_chip(now["across"])
            beside = to_core(now["across"])
            arrived += [other, beside]
            self.put("core", other, (now["across"], beside, meta["across"]))
        if "core" in now:
            other = to_core(now["core"])
            arrived.append(other)
            own, beside, info = meta["core"]
            self.writes.append(([own, now["core"], beside, other], info))
        for pieces, (name, row, quarter_rows, widths, row_by_core) in writes:
            self.fresh.append(name)
            self.outs[name] = place(
                self.outs.get(name), pieces, row, quarter_rows, widths, row_by_core
            )
        self.arrived = arrived
        return values if len(values) != 1 else values[0]


def tie(*values):
    return lax.optimization_barrier(values)


def on_device(
    inputs,
    skip_mask,
    block_order,
    norm1_gain,
    query_weight,
    key_weight,
    value_weight,
    w_out,
    norm2_gain,
    w_gate,
    w_up,
    w_down,
    out_grad,
):
    tensor_count = lax.axis_size("tensor")
    tensor_rank = lax.axis_index("tensor")
    seq_rank = lax.axis_index("seq")
    me = lax.axis_index("dp")
    chip, core = me // 2, me % 2
    micro, _, length, width = inputs.shape
    rows = micro * length
    slice_width = width // tensor_count
    core_half = width // 2
    block_rows = length // 2
    col_start = tensor_rank * slice_width

    def mine(values):
        return lax.dynamic_slice_in_dim(values, col_start, slice_width, values.ndim - 1)

    def scatter_tensor(part):
        if tensor_count != 2:
            sent = part.astype(BF)
            got = lax.psum_scatter(sent, "tensor", scatter_dimension=1, tiled=True)
            return got.astype(F32)
        sent = lax.dynamic_slice_in_dim(
            part, (1 - tensor_rank) * slice_width, slice_width, 1
        ).astype(BF)
        return mine(part) + swap_tensor(sent)

    gain_one = norm1_gain.astype(F32)
    gain_two = norm2_gain.astype(F32)
    gain_one_s = mine(gain_one)

    x_in = inputs.reshape(rows, width)
    g_in = out_grad.reshape(rows, width)
    in_f = x_in.astype(F32)
    active = jnp.repeat((1 - skip_mask[:, 0]).astype(F32), length)[:, None]
    offsets = jnp.arange(block_rows, dtype=jnp.int32)
    order = block_order[:, 0]
    key_pos = (order[:, :, None] * block_rows + offsets).reshape(micro, 1, -1)
    my_blocks = lax.dynamic_slice_in_dim(order, 2 * seq_rank, 2, 1)
    query_pos = (my_blocks[:, :, None] * block_rows + offsets).reshape(rows, 1)
    cos, sin = tables(query_pos[:, 0])

    scale_one = lax.rsqrt(jnp.mean(in_f * in_f, axis=-1, keepdims=True) + EPSILON)
    hn1 = (in_f * scale_one * gain_one).astype(BF)
    df = (active * g_in.astype(F32)).astype(BF)
    kvb = keys_and_values(hn1, key_weight, value_weight, cos, sin)
    kvb, hn1, df = tie(kvb, hn1, df)

    kv_all = lax.all_gather(kvb.reshape(micro, length, -1), "seq", axis=1, tiled=True)
    hn1_other = to_chip(hn1)
    df_other = to_chip(df)
    q = queries(hn1, query_weight, cos, sin)
    dz = dot_t(df, w_down)
    kv_all, hn1_other, df_other, q, dz, hn1, df = tie(kv_all, hn1_other, df_other, q, dz, hn1, df)

    def by_core(own, other):
        both = jnp.concatenate([own, other], axis=0)
        return jnp.concatenate([half(both, core), to_core(half(both, 1 - core))], axis=0)

    def by_chip(own, other):
        both = jnp.concatenate([own, other], axis=0)
        return jnp.concatenate([both, to_core(both)], axis=0)

    attended = []
    parts = []
    others = []
    for m in range(micro):
        o = attention(m, length, q, kv_all[m], query_pos, key_pos)
        attended.append(o)
        part = dot(o, w_out).astype(BF)
        parts.append(part)
        others.append(swap_tensor(part))
    hn1_core = by_core(hn1, hn1_other)
    df_core = by_core(df, df_other)
    mixed = jnp.concatenate([a.astype(F32) + b for a, b in zip(parts, others)], axis=0)
    ob = jnp.concatenate(attended, axis=0)
    hidden = in_f + active * mixed
    scale_two = lax.rsqrt(jnp.mean(hidden * hidden, axis=-1, keepdims=True) + EPSILON)
    hn2 = (hidden * scale_two * gain_two).astype(BF)
    hn2, hidden, scale_two, hn1_core, df_core = tie(hn2, hidden, scale_two, hn1_core, df_core)

    hn2_other = to_chip(hn2)
    g = dot(hn2, w_gate)
    u = dot(hn2, w_up)
    sig = jax.nn.sigmoid(g)
    silu = g * sig
    z = (silu * u).astype(BF)
    dg = (dz * u * sig * (1.0 + g * (1.0 - sig))).astype(BF)
    du = (dz * silu).astype(BF)
    z, dg, du = tie(z, dg, du)

    z_other = to_chip(half(z, 1 - chip))
    dn2_part = (dot_t(dg, w_gate) + dot_t(du, w_up)).astype(BF)
    z_other, dn2_part, hn2_other, dg, du = tie(z_other, dn2_part, hn2_other, dg, du)

    dn2_other = swap_tensor(dn2_part)
    z_chip = by_chip(half(z, chip), z_other)
    hn2_core = by_core(hn2, hn2_other)
    dgu_other = to_chip(jnp.concatenate([half(dg, 1 - chip), half(du, 1 - chip)], axis=1))
    down_quarter = dot_rows(z_chip, df_core)
    down_quarter, hn2_core = tie(down_quarter, hn2_core)
    down_part = lax.psum_scatter(down_quarter, "seq", scatter_dimension=0, tiled=True)
    dn2_other, dgu_other = tie(dn2_other, dgu_other)

    dgu = jnp.concatenate([half(dg, chip), half(du, chip)], axis=1)
    dgu_chip = by_chip(dgu, dgu_other)
    gate_up_quarter = dot_rows(hn2_core, dgu_chip)
    gate_up_part = lax.psum_scatter(gate_up_quarter, "seq", scatter_dimension=0, tiled=True)

    dn2 = dn2_part.astype(F32) + dn2_other
    grad_f = g_in.astype(F32)
    d_scaled = dn2 * gain_two
    inner_two = jnp.mean(d_scaled * hidden, axis=-1, keepdims=True)
    dh = grad_f + scale_two * d_scaled - hidden * scale_two**3 * inner_two
    gain_terms = mine(jnp.sum(dn2 * hidden * scale_two, axis=0))
    da = (active * dh).astype(BF)
    do = dot_t(da, w_out).astype(BF)
    da_other = to_chip(da)
    o_other = to_chip(half(ob, 1 - chip))
    dqs = []
    dkvs = []
    for m in range(micro):
        dq, dkv = attention(m, length, q, kv_all[m], query_pos, key_pos, do, cos, sin)
        dqs.append(dq)
        dkvs.append(dkv)
    dqb = jnp.concatenate(dqs, axis=0)
    dkvs, dqb, da_other, o_other, down_part = tie(
        jnp.stack(dkvs), dqb, da_other, o_other, down_part
    )

    dkv = lax.psum_scatter(dkvs, "seq", scatter_dimension=1, tiled=True)
    dq_part = dot_t(dqb, query_weight)
    branch = scatter_tensor(dot(z, w_down))
    da_core = by_core(da, da_other)
    o_chip = by_chip(half(ob, chip), o_other)
    out_quarter = dot_rows(o_chip, da_core)
    output = (mine(hidden) + active * branch).astype(BF)
    dkv, dq_part, out_quarter, output = tie(dkv, dq_part, out_quarter, output)

    chain = Chain()
    chain.add("out", out_quarter, 1, (core_half,), False)
    dkb, dvb = turn_back(dkv.reshape(rows, -1), cos, sin)
    grads = (dqb, dkb, dvb)
    widths = tuple(a.shape[1] // 2 for a in grads)
    qkv_other = to_chip(jnp.concatenate([half(a, 1 - chip) for a in grads], axis=1))
    qkv_own = jnp.concatenate([half(a, chip) for a in grads], axis=1)
    dn1 = dq_part + dot_t(dkb, key_weight) + dot_t(dvb, value_weight)
    qkv_other, qkv_own, dn1 = chain.tick(qkv_other, qkv_own, dn1)
    qkv_chip = by_chip(qkv_own, qkv_other)
    qkv_quarter = dot_rows(hn1_core, qkv_chip)
    dn1 = scatter_tensor(dn1)
    qkv_quarter, dn1 = chain.tick(qkv_quarter, dn1)
    chain.add("qkv", qkv_quarter, QKV_CHUNKS, widths, True)

    d_scaled_one = dn1 * gain_one_s
    in_slice = mine(in_f)
    inner_own = jnp.sum(d_scaled_one * in_slice, axis=-1)
    gains = jnp.stack([jnp.sum(dn1 * in_slice * scale_one, axis=0), gain_terms])
    inner_own, gains, d_scaled_one = chain.tick(inner_own, gains, d_scaled_one)
    inner_one = (inner_own + swap_tensor(inner_own))[:, None]
    input_grad = (
        mine(dh) + scale_one * d_scaled_one - in_slice * scale_one**3 * (inner_one / width)
    )
    gains = gains + to_chip(gains)
    gains, input_grad = chain.tick(gains, input_grad)
    gains = gains + to_core(gains)
    gains = chain.tick(gains)
    gains = gains + lax.ppermute(gains, "seq", PAIRS)
    gains = chain.tick(gains)
    gains = gains + lax.ppermute(gains, "seq", [(0, 2), (2, 0), (1, 3), (3, 1)])
    gains = chain.tick(gains)
    while chain.busy():
        chain.tick()

    gate_up = lax.all_gather(gate_up_part, ("dp", "seq"), axis=0, tiled=False)
    half_ff = z.shape[1] // 2
    gate, up = write_whole(gate_up, [(gate_up_part.shape[0], (half_ff, half_ff), True)])
    down_part, _ = tie(down_part, gate_up_part)
    every = lax.all_gather(down_part, ("dp", "seq"), axis=0, tiled=False)
    (down,) = write_whole(every, [(down_part.shape[0], (core_half,), False)])

    return (
        output.reshape(micro, 1, length, slice_width),
        input_grad.reshape(micro, 1, length, slice_width),
        gains[0],
        *chain.outs["qkv"],
        chain.outs["out"][0],
        gains[1],
        gate,
        up,
        down,
    )


def solution(mesh):
    return jax.shard_map(
        on_device,
        mesh=mesh,
        in_specs=(
            P(None, "dp", "seq", None),
            P(None, "dp"),
            P(None, "dp", None),
            P(),
            P(None, "tensor"),
            P(None, "tensor"),
            P(None, "tensor"),
            P("tensor", None),
            P(),
            P(None, "tensor"),
            P(None, "tensor"),
            P("tensor", None),
            P(None, "dp", "seq", None),
        ),
        out_specs=(
            P(None, "dp", "seq", "tensor"),
            P(None, "dp", "seq", "tensor"),
            P("tensor"),
            P(None, "tensor"),
            P(None, "tensor"),
            P(None, "tensor"),
            P("tensor", None),
            P("tensor"),
            P(None, "tensor"),
            P(None, "tensor"),
            P("tensor", None),
        ),
        check_vma=False,
    )
```

```python
import functools

import jax
import jax.numpy as jnp
from jax import lax
from jax.experimental import pallas as pl
from jax.experimental.pallas import tpu as pltpu
from jax.sharding import PartitionSpec as P

HEAD_DIMENSION = 128
EPSILON = 1e-05
NEGATIVE = -1e30
BF = jnp.bfloat16
F32 = jnp.float32
ACROSS = [(0, 2), (2, 0), (1, 3), (3, 1)]
CORES = [(0, 1), (1, 0), (2, 3), (3, 2)]
PAIRS = [(0, 1), (1, 0), (2, 3), (3, 2)]


def dot(a, b):
    return jnp.dot(a, b, preferred_element_type=F32)


def dot_t(a, b):
    return lax.dot_general(a, b, (((1,), (1,)), ((), ())), preferred_element_type=F32)


def dot_rows(a, b):
    out = lax.dot_general(a, b, (((0,), (0,)), ((), ())), preferred_element_type=F32)
    return out.astype(BF)


def swap_tensor(sent):
    if lax.axis_size("tensor") == 2:
        return lax.ppermute(sent, "tensor", [(0, 1), (1, 0)]).astype(F32)
    return lax.psum(sent.astype(F32), "tensor") - sent.astype(F32)


def half(values, index):
    width = values.shape[1] // 2
    return lax.dynamic_slice_in_dim(values, index * width, width, 1)


def to_core(sent):
    return lax.ppermute(sent, "dp", CORES)


def to_chip(sent):
    return lax.ppermute(sent, "dp", ACROSS)


def tables(positions):
    half_width = HEAD_DIMENSION // 2
    frequency = jnp.exp(
        jnp.arange(half_width, dtype=F32) * (-2.0 / HEAD_DIMENSION) * jnp.log(10000.0)
    )
    phases = positions.astype(F32)[:, None] * frequency[None, :]
    cos, sin = jnp.cos(phases), jnp.sin(phases)
    return jnp.concatenate([cos, cos], axis=1), jnp.concatenate([-sin, sin], axis=1)


def turn(values, cos, sin):
    return values * cos + pltpu.roll(values, HEAD_DIMENSION // 2, 1) * sin


def key_value_kernel(x_ref, key_ref, value_ref, cos_ref, sin_ref, out_ref):
    x = x_ref[...]
    keys = turn(dot(x, key_ref[...]), cos_ref[...], sin_ref[...])
    out_ref[:, :HEAD_DIMENSION] = keys.astype(BF)
    out_ref[:, HEAD_DIMENSION:] = dot(x, value_ref[...]).astype(BF)


def keys_and_values(x, key_weight, value_weight, cos, sin):
    rows, width = x.shape
    heads = key_weight.shape[1] // HEAD_DIMENSION
    whole = lambda step: (0, 0)
    column = lambda step: (0, step)
    return pl.pallas_call(
        key_value_kernel,
        grid=(heads,),
        in_specs=[
            pl.BlockSpec((rows, width), whole),
            pl.BlockSpec((width, HEAD_DIMENSION), column),
            pl.BlockSpec((width, HEAD_DIMENSION), column),
            pl.BlockSpec((rows, HEAD_DIMENSION), whole),
            pl.BlockSpec((rows, HEAD_DIMENSION), whole),
        ],
        out_specs=pl.BlockSpec((rows, 2 * HEAD_DIMENSION), column),
        out_shape=jax.ShapeDtypeStruct((rows, 2 * heads * HEAD_DIMENSION), BF),
        name="keys_and_values",
    )(x, key_weight, value_weight, cos, sin)


def query_kernel(x_ref, weight_ref, cos_ref, sin_ref, out_ref):
    raw = dot(x_ref[...], weight_ref[...])
    for start in range(0, raw.shape[1], HEAD_DIMENSION):
        head = raw[:, start : start + HEAD_DIMENSION]
        turned = turn(head, cos_ref[...], sin_ref[...])
        out_ref[:, start : start + HEAD_DIMENSION] = turned.astype(BF)


def queries(x, weight, cos, sin):
    rows, width = x.shape
    block = 2 * HEAD_DIMENSION
    whole = lambda step: (0, 0)
    column = lambda step: (0, step)
    return pl.pallas_call(
        query_kernel,
        grid=(weight.shape[1] // block,),
        in_specs=[
            pl.BlockSpec((rows, width), whole),
            pl.BlockSpec((width, block), column),
            pl.BlockSpec((rows, HEAD_DIMENSION), whole),
            pl.BlockSpec((rows, HEAD_DIMENSION), whole),
        ],
        out_specs=pl.BlockSpec((rows, block), column),
        out_shape=jax.ShapeDtypeStruct((rows, weight.shape[1]), BF),
        cost_estimate=pl.CostEstimate(
            flops=2 * rows * width * weight.shape[1],
            bytes_accessed=2 * width * weight.shape[1] + 2 * rows * width,
            transcendentals=0,
        ),
        name="queries",
    )(x, weight, cos, sin)


def probabilities(query, keys, query_pos, key_pos):
    scores = dot_t(query, keys) * HEAD_DIMENSION ** (-0.5)
    scores = jnp.where(key_pos <= query_pos, scores, NEGATIVE)
    expd = jnp.exp(scores - jnp.max(scores, axis=-1, keepdims=True))
    return expd / jnp.sum(expd, axis=-1, keepdims=True)


def attend_kernel(q_ref, kv_ref, query_pos_ref, key_pos_ref, out_ref):
    keys = kv_ref[:, :HEAD_DIMENSION]
    values = kv_ref[:, HEAD_DIMENSION:]
    for start in range(0, q_ref.shape[1], HEAD_DIMENSION):
        head = slice(start, start + HEAD_DIMENSION)
        prob = probabilities(q_ref[:, head], keys, query_pos_ref[...], key_pos_ref[...])
        out_ref[:, head] = dot(prob.astype(BF), values).astype(BF)


def attend_back_kernel(
    q_ref, kv_ref, query_pos_ref, key_pos_ref, do_ref, cos_ref, sin_ref, dq_ref, dkv_ref
):
    keys = kv_ref[:, :HEAD_DIMENSION]
    values = kv_ref[:, HEAD_DIMENSION:]
    dk = dv = None
    for start in range(0, q_ref.shape[1], HEAD_DIMENSION):
        head = slice(start, start + HEAD_DIMENSION)
        query = q_ref[:, head]
        do = do_ref[:, head]
        prob = probabilities(query, keys, query_pos_ref[...], key_pos_ref[...])
        dp = dot_t(do, values)
        inner = jnp.sum(prob * dp, axis=-1, keepdims=True)
        ds = (prob * (dp - inner) * HEAD_DIMENSION ** (-0.5)).astype(BF)
        dq = dot(ds, keys)
        dq_ref[:, head] = turn(dq, cos_ref[...], -sin_ref[...]).astype(BF)
        part_k = lax.dot_general(ds, query, (((0,), (0,)), ((), ())), preferred_element_type=F32)
        part_v = lax.dot_general(
            prob.astype(BF), do, (((0,), (0,)), ((), ())), preferred_element_type=F32
        )
        dk = part_k if dk is None else dk + part_k
        dv = part_v if dv is None else dv + part_v
    dkv_ref[:, :HEAD_DIMENSION] = dk.astype(BF)
    dkv_ref[:, HEAD_DIMENSION:] = dv.astype(BF)


def attention(m, length, q, kv_all, query_pos, key_pos, do=None, cos=None, sin=None):
    total = kv_all.shape[0]
    heads = kv_all.shape[1] // (2 * HEAD_DIMENSION)
    block = q.shape[1] // heads
    in_rows = lambda h: (m, h)
    column = lambda h: (0, h)
    in_specs = [
        pl.BlockSpec((length, block), in_rows),
        pl.BlockSpec((total, 2 * HEAD_DIMENSION), column),
        pl.BlockSpec((length, 1), lambda h: (m, 0)),
        pl.BlockSpec((None, 1, total), lambda h: (m, 0, 0)),
    ]
    operands = [q, kv_all, query_pos, key_pos]
    out_specs = pl.BlockSpec((length, block), column)
    out_shape = jax.ShapeDtypeStruct((length, q.shape[1]), BF)
    kernel = attend_kernel
    if do is not None:
        kernel = attend_back_kernel
        in_specs += [pl.BlockSpec((length, block), in_rows)]
        in_specs += [pl.BlockSpec((length, HEAD_DIMENSION), lambda h: (m, 0))] * 2
        operands += [do, cos, sin]
        out_specs = [out_specs, pl.BlockSpec((total, 2 * HEAD_DIMENSION), column)]
        out_shape = [out_shape, jax.ShapeDtypeStruct(kv_all.shape, BF)]
    return pl.pallas_call(
        kernel,
        grid=(heads,),
        in_specs=in_specs,
        out_specs=out_specs,
        out_shape=out_shape,
        cost_estimate=pl.CostEstimate(
            flops=(4 if do is None else 10) * length * total * q.shape[1],
            bytes_accessed=8 * kv_all.size,
            transcendentals=length * total * q.shape[1] // HEAD_DIMENSION,
        ),
        name="attend" if do is None else "attend_back",
    )(*operands)


def turn_back_kernel(dkv_ref, cos_ref, sin_ref, dk_ref, dv_ref):
    dk = dkv_ref[:, :HEAD_DIMENSION].astype(F32)
    dk_ref[...] = turn(dk, cos_ref[...], -sin_ref[...]).astype(BF)
    dv_ref[...] = dkv_ref[:, HEAD_DIMENSION:]


def turn_back(dkv, cos, sin):
    rows, both = dkv.shape
    column = lambda h: (0, h)
    return pl.pallas_call(
        turn_back_kernel,
        grid=(both // (2 * HEAD_DIMENSION),),
        in_specs=[pl.BlockSpec((rows, 2 * HEAD_DIMENSION), column)]
        + [pl.BlockSpec((rows, HEAD_DIMENSION), lambda h: (0, 0))] * 2,
        out_specs=[pl.BlockSpec((rows, HEAD_DIMENSION), column)] * 2,
        out_shape=[jax.ShapeDtypeStruct((rows, both // 2), BF)] * 2,
        name="turn_back",
    )(dkv, cos, sin)


def share_kernel(every_ref, *out_refs, pieces):
    out_refs = list(out_refs)
    for start, stop, widths in pieces:
        at = 0
        for width in widths:
            out_refs.pop(0)[...] = every_ref[start:stop, at : at + width].astype(F32)
            at += width


def write_whole(every, pieces):
    count, rows, cols = every.shape
    seq = lax.axis_size("seq")
    aligned = all(size % 16 == 0 and all(w % 128 == 0 for w in ws) for size, ws, _ in pieces)
    if not aligned:
        results = []
        start = 0
        for size, widths, row_by_core in pieces:
            at = 0
            for width in widths:
                piece = every[:, start : start + size, at : at + width]
                piece = piece.reshape(2, 2, seq, size, width)
                piece = piece.transpose((1, 2, 3, 0, 4) if row_by_core else (0, 2, 3, 1, 4))
                results.append(piece.reshape(2 * seq * size, 2 * width).astype(F32))
                at += width
            start += size
        return results
    spans = []
    out_specs = []
    out_shape = []
    start = 0
    for size, widths, row_by_core in pieces:
        spans.append((start, start + size, widths))

        def index(device, row_by_core=row_by_core):
            chip, core, rank = device // (2 * seq), (device // seq) % 2, device % seq
            row, column = (core, chip) if row_by_core else (chip, core)
            return row * seq + rank, column

        for width in widths:
            out_specs.append(pl.BlockSpec((size, width), index))
            out_shape.append(jax.ShapeDtypeStruct((2 * seq * size, 2 * width), F32))
        start += size
    return pl.pallas_call(
        functools.partial(share_kernel, pieces=tuple(spans)),
        grid=(count,),
        in_specs=[pl.BlockSpec((None, rows, cols), lambda device: (device, 0, 0))],
        out_specs=out_specs,
        out_shape=out_shape,
        cost_estimate=pl.CostEstimate(
            flops=0, bytes_accessed=6 * every.size, transcendentals=0
        ),
        name="write_whole",
    )(every)


def share(down_part, gate_up_part, out_quarter, qkv_quarter, widths):
    half_ff = gate_up_part.shape[1] // 2
    gate_up = lax.all_gather(gate_up_part, ("dp", "seq"), axis=0, tiled=False)
    gate, up = write_whole(gate_up, [(gate_up_part.shape[0], (half_ff, half_ff), True)])
    seq = lax.axis_size("seq")
    cols = out_quarter.shape[1]
    out_rows, qkv_rows = out_quarter.shape[0] // seq, qkv_quarter.shape[0] // seq
    down_rows = down_part.shape[0]
    if qkv_quarter.shape[1] == cols:
        joined = jnp.concatenate(
            [out_quarter.reshape(seq, out_rows, cols), qkv_quarter.reshape(seq, qkv_rows, cols)],
            axis=1,
        )
        part = lax.psum_scatter(joined, "seq", scatter_dimension=0, tiled=False)
        part = jnp.concatenate([down_part, part.reshape(out_rows + qkv_rows, cols)], axis=0)
        every = lax.all_gather(part, ("dp", "seq"), axis=0, tiled=False)
        down, out, query, key, value = write_whole(
            every,
            [(down_rows, (cols,), False), (out_rows, (cols,), False), (qkv_rows, widths, True)],
        )
    else:
        out_part = lax.psum_scatter(out_quarter, "seq", scatter_dimension=0, tiled=True)
        qkv_part = lax.psum_scatter(qkv_quarter, "seq", scatter_dimension=0, tiled=True)
        part = jnp.concatenate([down_part, out_part], axis=0)
        every = lax.all_gather(part, ("dp", "seq"), axis=0, tiled=False)
        down, out = write_whole(
            every, [(down_rows, (cols,), False), (out_rows, (cols,), False)]
        )
        every = lax.all_gather(qkv_part, ("dp", "seq"), axis=0, tiled=False)
        query, key, value = write_whole(every, [(qkv_rows, widths, True)])
    return dict(gate=gate, up=up, down=down, out=out, query=query, key=key, value=value)


def tie(*values):
    return lax.optimization_barrier(values)


def on_device(
    inputs,
    skip_mask,
    block_order,
    norm1_gain,
    query_weight,
    key_weight,
    value_weight,
    w_out,
    norm2_gain,
    w_gate,
    w_up,
    w_down,
    out_grad,
):
    tensor_count = lax.axis_size("tensor")
    tensor_rank = lax.axis_index("tensor")
    seq_rank = lax.axis_index("seq")
    me = lax.axis_index("dp")
    chip, core = me // 2, me % 2
    micro, _, length, width = inputs.shape
    rows = micro * length
    slice_width = width // tensor_count
    core_half = width // 2
    block_rows = length // 2
    col_start = tensor_rank * slice_width

    def mine(values):
        return lax.dynamic_slice_in_dim(values, col_start, slice_width, values.ndim - 1)

    def scatter_tensor(part):
        if tensor_count != 2:
            sent = part.astype(BF)
            got = lax.psum_scatter(sent, "tensor", scatter_dimension=1, tiled=True)
            return got.astype(F32)
        sent = lax.dynamic_slice_in_dim(
            part, (1 - tensor_rank) * slice_width, slice_width, 1
        ).astype(BF)
        return mine(part) + swap_tensor(sent)

    gain_one = norm1_gain.astype(F32)
    gain_two = norm2_gain.astype(F32)
    gain_one_s = mine(gain_one)

    x_in = inputs.reshape(rows, width)
    g_in = out_grad.reshape(rows, width)
    in_f = x_in.astype(F32)
    active = jnp.repeat((1 - skip_mask[:, 0]).astype(F32), length)[:, None]
    offsets = jnp.arange(block_rows, dtype=jnp.int32)
    order = block_order[:, 0]
    key_pos = (order[:, :, None] * block_rows + offsets).reshape(micro, 1, -1)
    my_blocks = lax.dynamic_slice_in_dim(order, 2 * seq_rank, 2, 1)
    query_pos = (my_blocks[:, :, None] * block_rows + offsets).reshape(rows, 1)
    cos, sin = tables(query_pos[:, 0])

    scale_one = lax.rsqrt(jnp.mean(in_f * in_f, axis=-1, keepdims=True) + EPSILON)
    hn1 = (in_f * scale_one * gain_one).astype(BF)
    df = (active * g_in.astype(F32)).astype(BF)
    kvb = keys_and_values(hn1, key_weight, value_weight, cos, sin)
    kvb, hn1, df = tie(kvb, hn1, df)

    kv_all = lax.all_gather(kvb.reshape(micro, length, -1), "seq", axis=1, tiled=True)
    hn1_other = to_chip(hn1)
    df_other = to_chip(df)
    q = queries(hn1, query_weight, cos, sin)
    dz = dot_t(df, w_down)
    kv_all, hn1_other, df_other, q, dz, hn1, df = tie(kv_all, hn1_other, df_other, q, dz, hn1, df)

    def by_core(own, other):
        both = jnp.concatenate([own, other], axis=0)
        return jnp.concatenate([half(both, core), to_core(half(both, 1 - core))], axis=0)

    def by_chip(own, other):
        both = jnp.concatenate([own, other], axis=0)
        return jnp.concatenate([both, to_core(both)], axis=0)

    attended = []
    parts = []
    others = []
    for m in range(micro):
        o = attention(m, length, q, kv_all[m], query_pos, key_pos)
        attended.append(o)
        part = dot(o, w_out).astype(BF)
        parts.append(part)
        others.append(swap_tensor(part))
    hn1_core = by_core(hn1, hn1_other)
    df_core = by_core(df, df_other)
    mixed = jnp.concatenate([a.astype(F32) + b for a, b in zip(parts, others)], axis=0)
    ob = jnp.concatenate(attended, axis=0)
    hidden = in_f + active * mixed
    scale_two = lax.rsqrt(jnp.mean(hidden * hidden, axis=-1, keepdims=True) + EPSILON)
    hn2 = (hidden * scale_two * gain_two).astype(BF)
    hn2, hidden, scale_two, hn1_core, df_core = tie(hn2, hidden, scale_two, hn1_core, df_core)

    g = dot(hn2, w_gate)
    u = dot(hn2, w_up)
    sig = jax.nn.sigmoid(g)
    silu = g * sig
    z = (silu * u).astype(BF)
    dg = (dz * u * sig * (1.0 + g * (1.0 - sig))).astype(BF)
    du = (dz * silu).astype(BF)
    z, dg, du = tie(z, dg, du)

    z_other = to_chip(half(z, 1 - chip))
    dn2_part = (dot_t(dg, w_gate) + dot_t(du, w_up)).astype(BF)
    z_other, dn2_part, dg, du, hn2 = tie(z_other, dn2_part, dg, du, hn2)
    hn2_other = to_chip(hn2)

    dn2_other = swap_tensor(dn2_part)
    z_chip = by_chip(half(z, chip), z_other)
    dgu_other = to_chip(jnp.concatenate([half(dg, 1 - chip), half(du, 1 - chip)], axis=1))
    down_quarter, hidden = tie(dot_rows(z_chip, df_core), hidden)
    down_part = lax.psum_scatter(down_quarter, "seq", scatter_dimension=0, tiled=True)
    dn2 = dn2_part.astype(F32) + dn2_other
    grad_f = g_in.astype(F32)
    d_scaled = dn2 * gain_two
    inner_two = jnp.mean(d_scaled * hidden, axis=-1, keepdims=True)
    dh = grad_f + scale_two * d_scaled - hidden * scale_two**3 * inner_two
    gain_terms = mine(jnp.sum(dn2 * hidden * scale_two, axis=0))
    da = (active * dh).astype(BF)
    do = dot_t(da, w_out).astype(BF)
    da_other = to_chip(da)
    o_other = to_chip(half(ob, 1 - chip))
    dqs = []
    dkvs = []
    for m in range(micro):
        dq, dkv = attention(m, length, q, kv_all[m], query_pos, key_pos, do, cos, sin)
        dqs.append(dq)
        dkvs.append(dkv)
    dqb = jnp.concatenate(dqs, axis=0)
    dkvs, dqb, hn2_other, dgu_other, down_part = tie(
        jnp.stack(dkvs), dqb, hn2_other, dgu_other, down_part
    )
    dkv = lax.psum_scatter(dkvs, "seq", scatter_dimension=1, tiled=True)

    hn2_core = by_core(hn2, hn2_other)
    dgu = jnp.concatenate([half(dg, chip), half(du, chip)], axis=1)
    dgu_chip = by_chip(dgu, dgu_other)
    gate_up_quarter = dot_rows(hn2_core, dgu_chip)
    dkv, da_other, o_other, gate_up_quarter = tie(dkv, da_other, o_other, gate_up_quarter)
    gate_up_part = lax.psum_scatter(gate_up_quarter, "seq", scatter_dimension=0, tiled=True)
    dq_part = dot_t(dqb, query_weight)
    branch = scatter_tensor(dot(z, w_down))
    da_core = by_core(da, da_other)
    o_chip = by_chip(half(ob, chip), o_other)
    out_quarter = dot_rows(o_chip, da_core)
    output = (mine(hidden) + active * branch).astype(BF)

    dkb, dvb = turn_back(dkv.reshape(rows, -1), cos, sin)
    grads = (dqb, dkb, dvb)
    widths = tuple(a.shape[1] // 2 for a in grads)
    qkv_other = to_chip(jnp.concatenate([half(a, 1 - chip) for a in grads], axis=1))
    qkv_own = jnp.concatenate([half(a, chip) for a in grads], axis=1)
    qkv_other, qkv_own = tie(qkv_other, qkv_own)
    qkv_chip = by_chip(qkv_own, qkv_other)
    qkv_quarter = dot_rows(hn1_core, qkv_chip)
    out_quarter, qkv_quarter, gate_up_part = tie(out_quarter, qkv_quarter, gate_up_part)
    results = share(down_part, gate_up_part, out_quarter, qkv_quarter, widths)

    dn1 = scatter_tensor(dq_part + dot_t(dkb, key_weight) + dot_t(dvb, value_weight))
    d_scaled_one = dn1 * gain_one_s
    in_slice = mine(in_f)
    inner_own = jnp.sum(d_scaled_one * in_slice, axis=-1)
    gains = jnp.stack([jnp.sum(dn1 * in_slice * scale_one, axis=0), gain_terms])
    inner_one = (inner_own + swap_tensor(inner_own))[:, None]
    input_grad = (
        mine(dh) + scale_one * d_scaled_one - in_slice * scale_one**3 * (inner_one / width)
    )
    gains = gains + to_chip(gains)
    gains = gains + to_core(gains)
    gains = gains + lax.ppermute(gains, "seq", PAIRS)
    gains = gains + lax.ppermute(gains, "seq", [(0, 2), (2, 0), (1, 3), (3, 1)])

    return (
        output.reshape(micro, 1, length, slice_width),
        input_grad.reshape(micro, 1, length, slice_width),
        gains[0],
        results["query"],
        results["key"],
        results["value"],
        results["out"],
        gains[1],
        results["gate"],
        results["up"],
        results["down"],
    )


def solution(mesh):
    return jax.shard_map(
        on_device,
        mesh=mesh,
        in_specs=(
            P(None, "dp", "seq", None),
            P(None, "dp"),
            P(None, "dp", None),
            P(),
            P(None, "tensor"),
            P(None, "tensor"),
            P(None, "tensor"),
            P("tensor", None),
            P(),
            P(None, "tensor"),
            P(None, "tensor"),
            P("tensor", None),
            P(None, "dp", "seq", None),
        ),
        out_specs=(
            P(None, "dp", "seq", "tensor"),
            P(None, "dp", "seq", "tensor"),
            P("tensor"),
            P(None, "tensor"),
            P(None, "tensor"),
            P(None, "tensor"),
            P("tensor", None),
            P("tensor"),
            P(None, "tensor"),
            P(None, "tensor"),
            P("tensor", None),
        ),
        check_vma=False,
    )
```

```python
import functools

import jax
import jax.numpy as jnp
from jax import lax
from jax.experimental import pallas as pl
from jax.experimental.pallas import tpu as pltpu
from jax.sharding import PartitionSpec as P

HEAD_DIMENSION = 128
EPSILON = 1e-05
NEGATIVE = -1e30
BF = jnp.bfloat16
F32 = jnp.float32
ACROSS = [(0, 2), (2, 0), (1, 3), (3, 1)]
CORES = [(0, 1), (1, 0), (2, 3), (3, 2)]
PAIRS = [(0, 1), (1, 0), (2, 3), (3, 2)]


def dot(a, b):
    return jnp.dot(a, b, preferred_element_type=F32)


def dot_t(a, b):
    return lax.dot_general(a, b, (((1,), (1,)), ((), ())), preferred_element_type=F32)


def dot_rows(a, b):
    out = lax.dot_general(a, b, (((0,), (0,)), ((), ())), preferred_element_type=F32)
    return out.astype(BF)


def swap_tensor(sent):
    if lax.axis_size("tensor") == 2:
        return lax.ppermute(sent, "tensor", [(0, 1), (1, 0)]).astype(F32)
    return lax.psum(sent.astype(F32), "tensor") - sent.astype(F32)


def half(values, index):
    width = values.shape[1] // 2
    return lax.dynamic_slice_in_dim(values, index * width, width, 1)


def to_core(sent):
    return lax.ppermute(sent, "dp", CORES)


def to_chip(sent):
    return lax.ppermute(sent, "dp", ACROSS)


def tables(positions):
    half_width = HEAD_DIMENSION // 2
    frequency = jnp.exp(
        jnp.arange(half_width, dtype=F32) * (-2.0 / HEAD_DIMENSION) * jnp.log(10000.0)
    )
    phases = positions.astype(F32)[:, None] * frequency[None, :]
    cos, sin = jnp.cos(phases), jnp.sin(phases)
    return jnp.concatenate([cos, cos], axis=1), jnp.concatenate([-sin, sin], axis=1)


def turn(values, cos, sin):
    return values * cos + pltpu.roll(values, HEAD_DIMENSION // 2, 1) * sin


def key_value_kernel(x_ref, key_ref, value_ref, cos_ref, sin_ref, out_ref):
    x = x_ref[...]
    keys = dot(x, key_ref[...])
    values = dot(x, value_ref[...]).astype(BF)
    for start in range(0, keys.shape[1], HEAD_DIMENSION):
        head = slice(start, start + HEAD_DIMENSION)
        turned = turn(keys[:, head], cos_ref[...], sin_ref[...])
        out_ref[:, 2 * start : 2 * start + HEAD_DIMENSION] = turned.astype(BF)
        out_ref[:, 2 * start + HEAD_DIMENSION : 2 * (start + HEAD_DIMENSION)] = values[:, head]


def keys_and_values(x, key_weight, value_weight, cos, sin):
    rows, width = x.shape
    columns = key_weight.shape[1]
    block = 2 * HEAD_DIMENSION if columns % (2 * HEAD_DIMENSION) == 0 else HEAD_DIMENSION
    whole = lambda step: (0, 0)
    column = lambda step: (0, step)
    return pl.pallas_call(
        key_value_kernel,
        grid=(columns // block,),
        in_specs=[
            pl.BlockSpec((rows, width), whole),
            pl.BlockSpec((width, block), column),
            pl.BlockSpec((width, block), column),
            pl.BlockSpec((rows, HEAD_DIMENSION), whole),
            pl.BlockSpec((rows, HEAD_DIMENSION), whole),
        ],
        out_specs=pl.BlockSpec((rows, 2 * block), column),
        out_shape=jax.ShapeDtypeStruct((rows, 2 * columns), BF),
        name="keys_and_values",
    )(x, key_weight, value_weight, cos, sin)


def query_kernel(x_ref, weight_ref, cos_ref, sin_ref, out_ref):
    raw = dot(x_ref[...], weight_ref[...])
    for start in range(0, raw.shape[1], HEAD_DIMENSION):
        head = raw[:, start : start + HEAD_DIMENSION]
        turned = turn(head, cos_ref[...], sin_ref[...])
        out_ref[:, start : start + HEAD_DIMENSION] = turned.astype(BF)


def queries(x, weight, cos, sin):
    rows, width = x.shape
    block = 2 * HEAD_DIMENSION
    whole = lambda step: (0, 0)
    column = lambda step: (0, step)
    return pl.pallas_call(
        query_kernel,
        grid=(weight.shape[1] // block,),
        in_specs=[
            pl.BlockSpec((rows, width), whole),
            pl.BlockSpec((width, block), column),
            pl.BlockSpec((rows, HEAD_DIMENSION), whole),
            pl.BlockSpec((rows, HEAD_DIMENSION), whole),
        ],
        out_specs=pl.BlockSpec((rows, block), column),
        out_shape=jax.ShapeDtypeStruct((rows, weight.shape[1]), BF),
        cost_estimate=pl.CostEstimate(
            flops=2 * rows * width * weight.shape[1],
            bytes_accessed=2 * width * weight.shape[1] + 2 * rows * width,
            transcendentals=0,
        ),
        name="queries",
    )(x, weight, cos, sin)


def probabilities(query, keys, query_pos, key_pos):
    scores = dot_t(query, keys) * HEAD_DIMENSION ** (-0.5)
    scores = jnp.where(key_pos <= query_pos, scores, NEGATIVE)
    expd = jnp.exp(scores - jnp.max(scores, axis=-1, keepdims=True))
    return expd / jnp.sum(expd, axis=-1, keepdims=True)


def attend_kernel(q_ref, kv_ref, query_pos_ref, key_pos_ref, out_ref):
    keys = kv_ref[:, :HEAD_DIMENSION]
    values = kv_ref[:, HEAD_DIMENSION:]
    for start in range(0, q_ref.shape[1], HEAD_DIMENSION):
        head = slice(start, start + HEAD_DIMENSION)
        prob = probabilities(q_ref[:, head], keys, query_pos_ref[...], key_pos_ref[...])
        out_ref[:, head] = dot(prob.astype(BF), values).astype(BF)


def attend_back_kernel(
    q_ref, kv_ref, query_pos_ref, key_pos_ref, do_ref, cos_ref, sin_ref, dq_ref, dkv_ref
):
    keys = kv_ref[:, :HEAD_DIMENSION]
    values = kv_ref[:, HEAD_DIMENSION:]
    dk = dv = None
    for start in range(0, q_ref.shape[1], HEAD_DIMENSION):
        head = slice(start, start + HEAD_DIMENSION)
        query = q_ref[:, head]
        do = do_ref[:, head]
        prob = probabilities(query, keys, query_pos_ref[...], key_pos_ref[...])
        dp = dot_t(do, values)
        inner = jnp.sum(prob * dp, axis=-1, keepdims=True)
        ds = (prob * (dp - inner) * HEAD_DIMENSION ** (-0.5)).astype(BF)
        dq = dot(ds, keys)
        dq_ref[:, head] = turn(dq, cos_ref[...], -sin_ref[...]).astype(BF)
        part_k = lax.dot_general(ds, query, (((0,), (0,)), ((), ())), preferred_element_type=F32)
        part_v = lax.dot_general(
            prob.astype(BF), do, (((0,), (0,)), ((), ())), preferred_element_type=F32
        )
        dk = part_k if dk is None else dk + part_k
        dv = part_v if dv is None else dv + part_v
    dkv_ref[:, :HEAD_DIMENSION] = dk.astype(BF)
    dkv_ref[:, HEAD_DIMENSION:] = dv.astype(BF)


def attention(m, length, q, kv_all, query_pos, key_pos, do=None, cos=None, sin=None):
    _, total, both = kv_all.shape
    heads = both // (2 * HEAD_DIMENSION)
    block = q.shape[1] // heads
    in_rows = lambda h: (m, h)
    column = lambda h: (0, h)
    in_specs = [
        pl.BlockSpec((length, block), in_rows),
        pl.BlockSpec((None, total, 2 * HEAD_DIMENSION), lambda h: (m, 0, h)),
        pl.BlockSpec((length, 1), lambda h: (m, 0)),
        pl.BlockSpec((None, 1, total), lambda h: (m, 0, 0)),
    ]
    operands = [q, kv_all, query_pos, key_pos]
    out_specs = pl.BlockSpec((length, block), column)
    out_shape = jax.ShapeDtypeStruct((length, q.shape[1]), BF)
    kernel = attend_kernel
    if do is not None:
        kernel = attend_back_kernel
        in_specs += [pl.BlockSpec((length, block), in_rows)]
        in_specs += [pl.BlockSpec((length, HEAD_DIMENSION), lambda h: (m, 0))] * 2
        operands += [do, cos, sin]
        out_specs = [out_specs, pl.BlockSpec((total, 2 * HEAD_DIMENSION), column)]
        out_shape = [out_shape, jax.ShapeDtypeStruct((total, both), BF)]
    return pl.pallas_call(
        kernel,
        grid=(heads,),
        in_specs=in_specs,
        out_specs=out_specs,
        out_shape=out_shape,
        cost_estimate=pl.CostEstimate(
            flops=(4 if do is None else 10) * length * total * q.shape[1],
            bytes_accessed=8 * total * both,
            transcendentals=length * total * q.shape[1] // HEAD_DIMENSION,
        ),
        name="attend" if do is None else "attend_back",
    )(*operands)


def turn_back_kernel(dkv_ref, cos_ref, sin_ref, dk_ref, dv_ref):
    dk = dkv_ref[:, :HEAD_DIMENSION].astype(F32)
    dk_ref[...] = turn(dk, cos_ref[...], -sin_ref[...]).astype(BF)
    dv_ref[...] = dkv_ref[:, HEAD_DIMENSION:]


def turn_back(dkv, cos, sin):
    rows, both = dkv.shape
    column = lambda h: (0, h)
    return pl.pallas_call(
        turn_back_kernel,
        grid=(both // (2 * HEAD_DIMENSION),),
        in_specs=[pl.BlockSpec((rows, 2 * HEAD_DIMENSION), column)]
        + [pl.BlockSpec((rows, HEAD_DIMENSION), lambda h: (0, 0))] * 2,
        out_specs=[pl.BlockSpec((rows, HEAD_DIMENSION), column)] * 2,
        out_shape=[jax.ShapeDtypeStruct((rows, both // 2), BF)] * 2,
        name="turn_back",
    )(dkv, cos, sin)


def share_kernel(every_ref, *out_refs, pieces):
    out_refs = list(out_refs)
    for start, stop, widths in pieces:
        size = stop - start
        at = 0
        for width in widths:
            out_ref = out_refs.pop(0)
            for i in range(every_ref.shape[0]):
                source = every_ref[i, start:stop, at : at + width]
                out_ref[i * size : (i + 1) * size, :] = source.astype(F32)
            at += width


def write_whole(every, pieces):
    count, rows, cols = every.shape
    seq = lax.axis_size("seq")
    aligned = all(size % 16 == 0 and all(w % 128 == 0 for w in ws) for size, ws, _ in pieces)
    if not aligned:
        results = []
        start = 0
        for size, widths, row_by_core in pieces:
            at = 0
            for width in widths:
                piece = every[:, start : start + size, at : at + width]
                piece = piece.reshape(2, 2, seq, size, width)
                piece = piece.transpose((1, 2, 3, 0, 4) if row_by_core else (0, 2, 3, 1, 4))
                results.append(piece.reshape(2 * seq * size, 2 * width).astype(F32))
                at += width
            start += size
        return results
    spans = []
    out_specs = []
    out_shape = []
    start = 0
    for size, widths, row_by_core in pieces:
        spans.append((start, start + size, widths))

        def index(device, row_by_core=row_by_core):
            chip, core = device // 2, device % 2
            return (core, chip) if row_by_core else (chip, core)

        for width in widths:
            out_specs.append(pl.BlockSpec((seq * size, width), index))
            out_shape.append(jax.ShapeDtypeStruct((2 * seq * size, 2 * width), F32))
        start += size
    return pl.pallas_call(
        functools.partial(share_kernel, pieces=tuple(spans)),
        grid=(count // seq,),
        in_specs=[pl.BlockSpec((seq, rows, cols), lambda device: (device, 0, 0))],
        out_specs=out_specs,
        out_shape=out_shape,
        cost_estimate=pl.CostEstimate(
            flops=0, bytes_accessed=6 * every.size, transcendentals=0
        ),
        compiler_params=pltpu.CompilerParams(vmem_limit_bytes=48 * 2**20),
        name="write_whole",
    )(every)


def share(down_part, gate_up_part, out_quarter, qkv_quarter, widths):
    half_ff = gate_up_part.shape[1] // 2
    gate_up = lax.all_gather(gate_up_part, ("dp", "seq"), axis=0, tiled=False)
    gate, up = write_whole(gate_up, [(gate_up_part.shape[0], (half_ff, half_ff), True)])
    seq = lax.axis_size("seq")
    cols = out_quarter.shape[1]
    out_rows, qkv_rows = out_quarter.shape[0] // seq, qkv_quarter.shape[0] // seq
    down_rows = down_part.shape[0]
    if qkv_quarter.shape[1] == cols:
        joined = jnp.concatenate(
            [out_quarter.reshape(seq, out_rows, cols), qkv_quarter.reshape(seq, qkv_rows, cols)],
            axis=1,
        )
        part = lax.psum_scatter(joined, "seq", scatter_dimension=0, tiled=False)
        part = jnp.concatenate([down_part, part.reshape(out_rows + qkv_rows, cols)], axis=0)
        every = lax.all_gather(part, ("dp", "seq"), axis=0, tiled=False)
        down, out, query, key, value = write_whole(
            every,
            [(down_rows, (cols,), False), (out_rows, (cols,), False), (qkv_rows, widths, True)],
        )
    else:
        out_part = lax.psum_scatter(out_quarter, "seq", scatter_dimension=0, tiled=True)
        qkv_part = lax.psum_scatter(qkv_quarter, "seq", scatter_dimension=0, tiled=True)
        part = jnp.concatenate([down_part, out_part], axis=0)
        every = lax.all_gather(part, ("dp", "seq"), axis=0, tiled=False)
        down, out = write_whole(
            every, [(down_rows, (cols,), False), (out_rows, (cols,), False)]
        )
        every = lax.all_gather(qkv_part, ("dp", "seq"), axis=0, tiled=False)
        query, key, value = write_whole(every, [(qkv_rows, widths, True)])
    return dict(gate=gate, up=up, down=down, out=out, query=query, key=key, value=value)


def tie(*values):
    return lax.optimization_barrier(values)


def on_device(
    inputs,
    skip_mask,
    block_order,
    norm1_gain,
    query_weight,
    key_weight,
    value_weight,
    w_out,
    norm2_gain,
    w_gate,
    w_up,
    w_down,
    out_grad,
):
    tensor_count = lax.axis_size("tensor")
    tensor_rank = lax.axis_index("tensor")
    seq_rank = lax.axis_index("seq")
    me = lax.axis_index("dp")
    chip, core = me // 2, me % 2
    micro, _, length, width = inputs.shape
    rows = micro * length
    slice_width = width // tensor_count
    core_half = width // 2
    block_rows = length // 2
    col_start = tensor_rank * slice_width

    def mine(values):
        return lax.dynamic_slice_in_dim(values, col_start, slice_width, values.ndim - 1)

    def scatter_tensor(part):
        if tensor_count != 2:
            sent = part.astype(BF)
            got = lax.psum_scatter(sent, "tensor", scatter_dimension=1, tiled=True)
            return got.astype(F32)
        sent = lax.dynamic_slice_in_dim(
            part, (1 - tensor_rank) * slice_width, slice_width, 1
        ).astype(BF)
        return mine(part) + swap_tensor(sent)

    gain_one = norm1_gain.astype(F32)
    gain_two = norm2_gain.astype(F32)
    gain_one_s = mine(gain_one)

    x_in = inputs.reshape(rows, width)
    g_in = out_grad.reshape(rows, width)
    in_f = x_in.astype(F32)
    active = jnp.repeat((1 - skip_mask[:, 0]).astype(F32), length)[:, None]
    offsets = jnp.arange(block_rows, dtype=jnp.int32)
    order = block_order[:, 0]
    key_pos = (order[:, :, None] * block_rows + offsets).reshape(micro, 1, -1)
    my_blocks = lax.dynamic_slice_in_dim(order, 2 * seq_rank, 2, 1)
    query_pos = (my_blocks[:, :, None] * block_rows + offsets).reshape(rows, 1)
    cos, sin = tables(query_pos[:, 0])

    scale_one = lax.rsqrt(jnp.mean(in_f * in_f, axis=-1, keepdims=True) + EPSILON)
    hn1 = (in_f * scale_one * gain_one).astype(BF)
    df = (active * g_in.astype(F32)).astype(BF)
    kvb = keys_and_values(hn1, key_weight, value_weight, cos, sin)
    kvb, hn1, df = tie(kvb, hn1, df)

    kv_all = lax.all_gather(kvb.reshape(micro, length, -1), "seq", axis=1, tiled=True)
    hn1_other = to_chip(hn1)
    df_other = to_chip(df)
    q = queries(hn1, query_weight, cos, sin)
    dz = dot_t(df, w_down)
    kv_all, q, dz = tie(kv_all, q, dz)

    def by_core(own, other):
        both = jnp.concatenate([own, other], axis=0)
        return jnp.concatenate([half(both, core), to_core(half(both, 1 - core))], axis=0)

    def by_chip(own, other):
        both = jnp.concatenate([own, other], axis=0)
        return jnp.concatenate([both, to_core(both)], axis=0)

    attended = []
    parts = []
    others = []
    for m in range(micro):
        o = attention(m, length, q, kv_all, query_pos, key_pos)
        attended.append(o)
        part = dot(o, w_out).astype(BF)
        parts.append(part)
        others.append(swap_tensor(part))
    hn1_other, df_other, attended[-1] = tie(hn1_other, df_other, attended[-1])
    hn1_core = by_core(hn1, hn1_other)
    df_core = by_core(df, df_other)
    mixed = jnp.concatenate([a.astype(F32) + b for a, b in zip(parts, others)], axis=0)
    ob = jnp.concatenate(attended, axis=0)
    hidden = in_f + active * mixed
    scale_two = lax.rsqrt(jnp.mean(hidden * hidden, axis=-1, keepdims=True) + EPSILON)
    hn2 = (hidden * scale_two * gain_two).astype(BF)
    hn2, hidden, scale_two, hn1_core, df_core = tie(hn2, hidden, scale_two, hn1_core, df_core)

    g = dot(hn2, w_gate)
    u = dot(hn2, w_up)
    sig = jax.nn.sigmoid(g)
    silu = g * sig
    z = (silu * u).astype(BF)
    dg = (dz * u * sig * (1.0 + g * (1.0 - sig))).astype(BF)
    du = (dz * silu).astype(BF)
    z, dg, du = tie(z, dg, du)

    z_other = to_chip(half(z, 1 - chip))
    dn2_part = (dot_t(dg, w_gate) + dot_t(du, w_up)).astype(BF)
    z_other, dn2_part, dg, du, hn2 = tie(z_other, dn2_part, dg, du, hn2)
    hn2_other = to_chip(hn2)

    dn2_other = swap_tensor(dn2_part)
    z_chip = by_chip(half(z, chip), z_other)
    dgu_other = to_chip(jnp.concatenate([half(dg, 1 - chip), half(du, 1 - chip)], axis=1))
    down_quarter, hidden = tie(dot_rows(z_chip, df_core), hidden)
    down_part = lax.psum_scatter(down_quarter, "seq", scatter_dimension=0, tiled=True)
    dn2 = dn2_part.astype(F32) + dn2_other
    grad_f = g_in.astype(F32)
    d_scaled = dn2 * gain_two
    inner_two = jnp.mean(d_scaled * hidden, axis=-1, keepdims=True)
    dh = grad_f + scale_two * d_scaled - hidden * scale_two**3 * inner_two
    gain_terms = mine(jnp.sum(dn2 * hidden * scale_two, axis=0))
    da = (active * dh).astype(BF)
    do = dot_t(da, w_out).astype(BF)
    da_other = to_chip(da)
    o_other = to_chip(half(ob, 1 - chip))
    dqs = []
    dkvs = []
    for m in range(micro):
        dq, dkv = attention(m, length, q, kv_all, query_pos, key_pos, do, cos, sin)
        dqs.append(dq)
        dkvs.append(dkv)
    dqb = jnp.concatenate(dqs, axis=0)
    dkvs, dqb, hn2_other, dgu_other, down_part = tie(
        jnp.stack(dkvs), dqb, hn2_other, dgu_other, down_part
    )
    dkv = lax.psum_scatter(dkvs, "seq", scatter_dimension=1, tiled=True)

    hn2_core = by_core(hn2, hn2_other)
    dgu = jnp.concatenate([half(dg, chip), half(du, chip)], axis=1)
    dgu_chip = by_chip(dgu, dgu_other)
    gate_up_quarter = dot_rows(hn2_core, dgu_chip)
    dkv, da_other, o_other, gate_up_quarter = tie(dkv, da_other, o_other, gate_up_quarter)
    gate_up_part = lax.psum_scatter(gate_up_quarter, "seq", scatter_dimension=0, tiled=True)
    dq_part = dot_t(dqb, query_weight)
    branch = scatter_tensor(dot(z, w_down))
    da_core = by_core(da, da_other)
    o_chip = by_chip(half(ob, chip), o_other)
    out_quarter = dot_rows(o_chip, da_core)
    output = (mine(hidden) + active * branch).astype(BF)

    dkb, dvb = turn_back(dkv.reshape(rows, -1), cos, sin)
    grads = (dqb, dkb, dvb)
    widths = tuple(a.shape[1] // 2 for a in grads)
    qkv_other = to_chip(jnp.concatenate([half(a, 1 - chip) for a in grads], axis=1))
    qkv_own = jnp.concatenate([half(a, chip) for a in grads], axis=1)
    qkv_other, qkv_own = tie(qkv_other, qkv_own)
    qkv_chip = by_chip(qkv_own, qkv_other)
    qkv_quarter = dot_rows(hn1_core, qkv_chip)
    out_quarter, qkv_quarter, gate_up_part = tie(out_quarter, qkv_quarter, gate_up_part)
    results = share(down_part, gate_up_part, out_quarter, qkv_quarter, widths)

    dn1 = scatter_tensor(dq_part + dot_t(dkb, key_weight) + dot_t(dvb, value_weight))
    d_scaled_one = dn1 * gain_one_s
    in_slice = mine(in_f)
    inner_own = jnp.sum(d_scaled_one * in_slice, axis=-1)
    gains = jnp.stack([jnp.sum(dn1 * in_slice * scale_one, axis=0), gain_terms])
    inner_one = (inner_own + swap_tensor(inner_own))[:, None]
    input_grad = (
        mine(dh) + scale_one * d_scaled_one - in_slice * scale_one**3 * (inner_one / width)
    )
    gains = gains + to_chip(gains)
    gains = gains + to_core(gains)
    gains = gains + lax.ppermute(gains, "seq", PAIRS)
    gains = gains + lax.ppermute(gains, "seq", [(0, 2), (2, 0), (1, 3), (3, 1)])

    return (
        output.reshape(micro, 1, length, slice_width),
        input_grad.reshape(micro, 1, length, slice_width),
        gains[0],
        results["query"],
        results["key"],
        results["value"],
        results["out"],
        gains[1],
        results["gate"],
        results["up"],
        results["down"],
    )


def solution(mesh):
    return jax.shard_map(
        on_device,
        mesh=mesh,
        in_specs=(
            P(None, "dp", "seq", None),
            P(None, "dp"),
            P(None, "dp", None),
            P(),
            P(None, "tensor"),
            P(None, "tensor"),
            P(None, "tensor"),
            P("tensor", None),
            P(),
            P(None, "tensor"),
            P(None, "tensor"),
            P("tensor", None),
            P(None, "dp", "seq", None),
        ),
        out_specs=(
            P(None, "dp", "seq", "tensor"),
            P(None, "dp", "seq", "tensor"),
            P("tensor"),
            P(None, "tensor"),
            P(None, "tensor"),
            P(None, "tensor"),
            P("tensor", None),
            P("tensor"),
            P(None, "tensor"),
            P(None, "tensor"),
            P("tensor", None),
        ),
        check_vma=False,
    )
```

```python
import functools

import jax
import jax.numpy as jnp
from jax import lax
from jax.experimental import pallas as pl
from jax.experimental.pallas import tpu as pltpu
from jax.sharding import PartitionSpec as P

HEAD_DIMENSION = 128
EPSILON = 1e-05
NEGATIVE = -1e30
BF = jnp.bfloat16
F32 = jnp.float32
ACROSS = [(0, 2), (2, 0), (1, 3), (3, 1)]
CORES = [(0, 1), (1, 0), (2, 3), (3, 2)]
PAIRS = [(0, 1), (1, 0), (2, 3), (3, 2)]


def dot(a, b):
    return jnp.dot(a, b, preferred_element_type=F32)


def dot_t(a, b):
    return lax.dot_general(a, b, (((1,), (1,)), ((), ())), preferred_element_type=F32)


def dot_rows(a, b):
    out = lax.dot_general(a, b, (((0,), (0,)), ((), ())), preferred_element_type=F32)
    return out.astype(BF)


def swap_tensor(sent):
    if lax.axis_size("tensor") == 2:
        return lax.ppermute(sent, "tensor", [(0, 1), (1, 0)]).astype(F32)
    return lax.psum(sent.astype(F32), "tensor") - sent.astype(F32)


def half(values, index):
    width = values.shape[1] // 2
    return lax.dynamic_slice_in_dim(values, index * width, width, 1)


def to_core(sent):
    return lax.ppermute(sent, "dp", CORES)


def to_chip(sent):
    return lax.ppermute(sent, "dp", ACROSS)


def tables(positions):
    half_width = HEAD_DIMENSION // 2
    frequency = jnp.exp(
        jnp.arange(half_width, dtype=F32) * (-2.0 / HEAD_DIMENSION) * jnp.log(10000.0)
    )
    phases = positions.astype(F32)[:, None] * frequency[None, :]
    cos, sin = jnp.cos(phases), jnp.sin(phases)
    return jnp.concatenate([cos, cos], axis=1), jnp.concatenate([-sin, sin], axis=1)


def turn(values, cos, sin):
    return values * cos + pltpu.roll(values, HEAD_DIMENSION // 2, 1) * sin


def key_value_kernel(x_ref, key_ref, value_ref, cos_ref, sin_ref, out_ref):
    x = x_ref[...]
    keys = dot(x, key_ref[...])
    values = dot(x, value_ref[...]).astype(BF)
    for start in range(0, keys.shape[1], HEAD_DIMENSION):
        head = slice(start, start + HEAD_DIMENSION)
        turned = turn(keys[:, head], cos_ref[...], sin_ref[...])
        out_ref[:, 2 * start : 2 * start + HEAD_DIMENSION] = turned.astype(BF)
        out_ref[:, 2 * start + HEAD_DIMENSION : 2 * (start + HEAD_DIMENSION)] = values[:, head]


def keys_and_values(x, key_weight, value_weight, cos, sin):
    rows, width = x.shape
    columns = key_weight.shape[1]
    block = 2 * HEAD_DIMENSION if columns % (2 * HEAD_DIMENSION) == 0 else HEAD_DIMENSION
    whole = lambda step: (0, 0)
    column = lambda step: (0, step)
    return pl.pallas_call(
        key_value_kernel,
        grid=(columns // block,),
        in_specs=[
            pl.BlockSpec((rows, width), whole),
            pl.BlockSpec((width, block), column),
            pl.BlockSpec((width, block), column),
            pl.BlockSpec((rows, HEAD_DIMENSION), whole),
            pl.BlockSpec((rows, HEAD_DIMENSION), whole),
        ],
        out_specs=pl.BlockSpec((rows, 2 * block), column),
        out_shape=jax.ShapeDtypeStruct((rows, 2 * columns), BF),
        name="keys_and_values",
    )(x, key_weight, value_weight, cos, sin)


def query_kernel(x_ref, weight_ref, cos_ref, sin_ref, out_ref):
    raw = dot(x_ref[...], weight_ref[...])
    for start in range(0, raw.shape[1], HEAD_DIMENSION):
        head = raw[:, start : start + HEAD_DIMENSION]
        turned = turn(head, cos_ref[...], sin_ref[...])
        out_ref[:, start : start + HEAD_DIMENSION] = turned.astype(BF)


def queries(x, weight, cos, sin):
    rows, width = x.shape
    block = 2 * HEAD_DIMENSION
    whole = lambda step: (0, 0)
    column = lambda step: (0, step)
    return pl.pallas_call(
        query_kernel,
        grid=(weight.shape[1] // block,),
        in_specs=[
            pl.BlockSpec((rows, width), whole),
            pl.BlockSpec((width, block), column),
            pl.BlockSpec((rows, HEAD_DIMENSION), whole),
            pl.BlockSpec((rows, HEAD_DIMENSION), whole),
        ],
        out_specs=pl.BlockSpec((rows, block), column),
        out_shape=jax.ShapeDtypeStruct((rows, weight.shape[1]), BF),
        cost_estimate=pl.CostEstimate(
            flops=2 * rows * width * weight.shape[1],
            bytes_accessed=2 * width * weight.shape[1] + 2 * rows * width,
            transcendentals=0,
        ),
        name="queries",
    )(x, weight, cos, sin)


def probabilities(query, keys, query_pos, key_pos):
    scores = dot_t(query, keys) * HEAD_DIMENSION ** (-0.5)
    scores = jnp.where(key_pos <= query_pos, scores, NEGATIVE)
    expd = jnp.exp(scores - jnp.max(scores, axis=-1, keepdims=True))
    return expd / jnp.sum(expd, axis=-1, keepdims=True)


def attend_kernel(q_ref, kv_ref, query_pos_ref, key_pos_ref, out_ref):
    keys = kv_ref[:, :HEAD_DIMENSION]
    values = kv_ref[:, HEAD_DIMENSION:]
    for start in range(0, q_ref.shape[1], HEAD_DIMENSION):
        head = slice(start, start + HEAD_DIMENSION)
        prob = probabilities(q_ref[:, head], keys, query_pos_ref[...], key_pos_ref[...])
        out_ref[:, head] = dot(prob.astype(BF), values).astype(BF)


def attend_back_kernel(
    q_ref, kv_ref, query_pos_ref, key_pos_ref, do_ref, cos_ref, sin_ref, dq_ref, dkv_ref
):
    keys = kv_ref[:, :HEAD_DIMENSION]
    values = kv_ref[:, HEAD_DIMENSION:]
    dk = dv = None
    for start in range(0, q_ref.shape[1], HEAD_DIMENSION):
        head = slice(start, start + HEAD_DIMENSION)
        query = q_ref[:, head]
        do = do_ref[:, head]
        prob = probabilities(query, keys, query_pos_ref[...], key_pos_ref[...])
        dp = dot_t(do, values)
        inner = jnp.sum(prob * dp, axis=-1, keepdims=True)
        ds = (prob * (dp - inner) * HEAD_DIMENSION ** (-0.5)).astype(BF)
        dq = dot(ds, keys)
        dq_ref[:, head] = turn(dq, cos_ref[...], -sin_ref[...]).astype(BF)
        part_k = lax.dot_general(ds, query, (((0,), (0,)), ((), ())), preferred_element_type=F32)
        part_v = lax.dot_general(
            prob.astype(BF), do, (((0,), (0,)), ((), ())), preferred_element_type=F32
        )
        dk = part_k if dk is None else dk + part_k
        dv = part_v if dv is None else dv + part_v
    dkv_ref[:, :HEAD_DIMENSION] = dk.astype(BF)
    dkv_ref[:, HEAD_DIMENSION:] = dv.astype(BF)


def attention(m, length, q, kv_all, query_pos, key_pos, do=None, cos=None, sin=None):
    _, total, both = kv_all.shape
    heads = both // (2 * HEAD_DIMENSION)
    block = q.shape[1] // heads
    in_rows = lambda h: (m, h)
    column = lambda h: (0, h)
    in_specs = [
        pl.BlockSpec((length, block), in_rows),
        pl.BlockSpec((None, total, 2 * HEAD_DIMENSION), lambda h: (m, 0, h)),
        pl.BlockSpec((length, 1), lambda h: (m, 0)),
        pl.BlockSpec((None, 1, total), lambda h: (m, 0, 0)),
    ]
    operands = [q, kv_all, query_pos, key_pos]
    out_specs = pl.BlockSpec((length, block), column)
    out_shape = jax.ShapeDtypeStruct((length, q.shape[1]), BF)
    kernel = attend_kernel
    if do is not None:
        kernel = attend_back_kernel
        in_specs += [pl.BlockSpec((length, block), in_rows)]
        in_specs += [pl.BlockSpec((length, HEAD_DIMENSION), lambda h: (m, 0))] * 2
        operands += [do, cos, sin]
        out_specs = [out_specs, pl.BlockSpec((total, 2 * HEAD_DIMENSION), column)]
        out_shape = [out_shape, jax.ShapeDtypeStruct((total, both), BF)]
    return pl.pallas_call(
        kernel,
        grid=(heads,),
        in_specs=in_specs,
        out_specs=out_specs,
        out_shape=out_shape,
        cost_estimate=pl.CostEstimate(
            flops=(4 if do is None else 10) * length * total * q.shape[1],
            bytes_accessed=8 * total * both,
            transcendentals=length * total * q.shape[1] // HEAD_DIMENSION,
        ),
        name="attend" if do is None else "attend_back",
    )(*operands)


def turn_back_kernel(dkv_ref, cos_ref, sin_ref, dk_ref, dv_ref):
    dk = dkv_ref[:, :HEAD_DIMENSION].astype(F32)
    dk_ref[...] = turn(dk, cos_ref[...], -sin_ref[...]).astype(BF)
    dv_ref[...] = dkv_ref[:, HEAD_DIMENSION:]


def turn_back(dkv, cos, sin):
    rows, both = dkv.shape
    column = lambda h: (0, h)
    return pl.pallas_call(
        turn_back_kernel,
        grid=(both // (2 * HEAD_DIMENSION),),
        in_specs=[pl.BlockSpec((rows, 2 * HEAD_DIMENSION), column)]
        + [pl.BlockSpec((rows, HEAD_DIMENSION), lambda h: (0, 0))] * 2,
        out_specs=[pl.BlockSpec((rows, HEAD_DIMENSION), column)] * 2,
        out_shape=[jax.ShapeDtypeStruct((rows, both // 2), BF)] * 2,
        name="turn_back",
    )(dkv, cos, sin)


def share_kernel(every_ref, *out_refs, pieces):
    out_refs = list(out_refs)
    for start, stop, widths in pieces:
        size = stop - start
        at = 0
        for width in widths:
            out_ref = out_refs.pop(0)
            for i in range(every_ref.shape[0]):
                source = every_ref[i, start:stop, at : at + width]
                out_ref[i * size : (i + 1) * size, :] = source.astype(F32)
            at += width


def write_whole(every, pieces):
    count, rows, cols = every.shape
    seq = lax.axis_size("seq")
    aligned = all(size % 16 == 0 and all(w % 128 == 0 for w in ws) for size, ws, _ in pieces)
    if not aligned:
        results = []
        start = 0
        for size, widths, row_by_core in pieces:
            at = 0
            for width in widths:
                piece = every[:, start : start + size, at : at + width]
                piece = piece.reshape(seq, 2, 2, size, width)
                piece = piece.transpose((2, 0, 3, 1, 4) if row_by_core else (1, 0, 3, 2, 4))
                results.append(piece.reshape(2 * seq * size, 2 * width).astype(F32))
                at += width
            start += size
        return results
    spans = []
    out_specs = []
    out_shape = []
    start = 0
    for size, widths, row_by_core in pieces:
        spans.append((start, start + size, widths))

        def index(device, row_by_core=row_by_core):
            chip, core = device // 2, device % 2
            return (core, chip) if row_by_core else (chip, core)

        for width in widths:
            out_specs.append(pl.BlockSpec((seq * size, width), index))
            out_shape.append(jax.ShapeDtypeStruct((2 * seq * size, 2 * width), F32))
        start += size
    return pl.pallas_call(
        functools.partial(share_kernel, pieces=tuple(spans)),
        grid=(count // seq,),
        in_specs=[pl.BlockSpec((seq, None, rows, cols), lambda device: (0, device, 0, 0))],
        out_specs=out_specs,
        out_shape=out_shape,
        cost_estimate=pl.CostEstimate(
            flops=0, bytes_accessed=6 * every.size, transcendentals=0
        ),
        compiler_params=pltpu.CompilerParams(vmem_limit_bytes=48 * 2**20),
        name="write_whole",
    )(every.reshape(seq, count // seq, rows, cols))


def share(down_part, gate_up_part, out_quarter, qkv_quarter, widths):
    half_ff = gate_up_part.shape[1] // 2
    gate_up = lax.all_gather(gate_up_part, ("seq", "dp"), axis=0, tiled=False)
    gate, up = write_whole(gate_up, [(gate_up_part.shape[0], (half_ff, half_ff), True)])
    seq = lax.axis_size("seq")
    cols = out_quarter.shape[1]
    out_rows, qkv_rows = out_quarter.shape[0] // seq, qkv_quarter.shape[0] // seq
    down_rows = down_part.shape[0]
    if qkv_quarter.shape[1] == cols:
        joined = jnp.concatenate(
            [out_quarter.reshape(seq, out_rows, cols), qkv_quarter.reshape(seq, qkv_rows, cols)],
            axis=1,
        )
        part = lax.psum_scatter(joined, "seq", scatter_dimension=0, tiled=False)
        part = jnp.concatenate([down_part, part.reshape(out_rows + qkv_rows, cols)], axis=0)
        every = lax.all_gather(part, ("seq", "dp"), axis=0, tiled=False)
        down, out, query, key, value = write_whole(
            every,
            [(down_rows, (cols,), False), (out_rows, (cols,), False), (qkv_rows, widths, True)],
        )
    else:
        out_part = lax.psum_scatter(out_quarter, "seq", scatter_dimension=0, tiled=True)
        qkv_part = lax.psum_scatter(qkv_quarter, "seq", scatter_dimension=0, tiled=True)
        part = jnp.concatenate([down_part, out_part], axis=0)
        every = lax.all_gather(part, ("seq", "dp"), axis=0, tiled=False)
        down, out = write_whole(
            every, [(down_rows, (cols,), False), (out_rows, (cols,), False)]
        )
        every = lax.all_gather(qkv_part, ("seq", "dp"), axis=0, tiled=False)
        query, key, value = write_whole(every, [(qkv_rows, widths, True)])
    return dict(gate=gate, up=up, down=down, out=out, query=query, key=key, value=value)


def tie(*values):
    return lax.optimization_barrier(values)


def on_device(
    inputs,
    skip_mask,
    block_order,
    norm1_gain,
    query_weight,
    key_weight,
    value_weight,
    w_out,
    norm2_gain,
    w_gate,
    w_up,
    w_down,
    out_grad,
):
    tensor_count = lax.axis_size("tensor")
    tensor_rank = lax.axis_index("tensor")
    seq_rank = lax.axis_index("seq")
    me = lax.axis_index("dp")
    chip, core = me // 2, me % 2
    micro, _, length, width = inputs.shape
    rows = micro * length
    slice_width = width // tensor_count
    core_half = width // 2
    block_rows = length // 2
    col_start = tensor_rank * slice_width

    def mine(values):
        return lax.dynamic_slice_in_dim(values, col_start, slice_width, values.ndim - 1)

    def scatter_tensor(part):
        if tensor_count != 2:
            sent = part.astype(BF)
            got = lax.psum_scatter(sent, "tensor", scatter_dimension=1, tiled=True)
            return got.astype(F32)
        sent = lax.dynamic_slice_in_dim(
            part, (1 - tensor_rank) * slice_width, slice_width, 1
        ).astype(BF)
        return mine(part) + swap_tensor(sent)

    gain_one = norm1_gain.astype(F32)
    gain_two = norm2_gain.astype(F32)
    gain_one_s = mine(gain_one)

    x_in = inputs.reshape(rows, width)
    g_in = out_grad.reshape(rows, width)
    in_f = x_in.astype(F32)
    active = jnp.repeat((1 - skip_mask[:, 0]).astype(F32), length)[:, None]
    offsets = jnp.arange(block_rows, dtype=jnp.int32)
    order = block_order[:, 0]
    key_pos = (order[:, :, None] * block_rows + offsets).reshape(micro, 1, -1)
    my_blocks = lax.dynamic_slice_in_dim(order, 2 * seq_rank, 2, 1)
    query_pos = (my_blocks[:, :, None] * block_rows + offsets).reshape(rows, 1)
    cos, sin = tables(query_pos[:, 0])

    scale_one = lax.rsqrt(jnp.mean(in_f * in_f, axis=-1, keepdims=True) + EPSILON)
    hn1 = (in_f * scale_one * gain_one).astype(BF)
    df = (active * g_in.astype(F32)).astype(BF)
    kvb = keys_and_values(hn1, key_weight, value_weight, cos, sin)
    kvb, hn1, df = tie(kvb, hn1, df)

    kv_all = lax.all_gather(kvb.reshape(micro, length, -1), "seq", axis=1, tiled=True)
    hn1_other = to_chip(hn1)
    df_other = to_chip(df)
    q = queries(hn1, query_weight, cos, sin)
    dz = dot_t(df, w_down)
    kv_all, q, dz = tie(kv_all, q, dz)

    def by_core(own, other):
        both = jnp.concatenate([own, other], axis=0)
        return jnp.concatenate([half(both, core), to_core(half(both, 1 - core))], axis=0)

    def by_chip(own, other):
        both = jnp.concatenate([own, other], axis=0)
        return jnp.concatenate([both, to_core(both)], axis=0)

    attended = []
    parts = []
    others = []
    for m in range(micro):
        o = attention(m, length, q, kv_all, query_pos, key_pos)
        attended.append(o)
        part = dot(o, w_out).astype(BF)
        parts.append(part)
        others.append(swap_tensor(part))
    hn1_other, df_other, attended[-1] = tie(hn1_other, df_other, attended[-1])
    hn1_core = by_core(hn1, hn1_other)
    df_core = by_core(df, df_other)
    mixed = jnp.concatenate([a.astype(F32) + b for a, b in zip(parts, others)], axis=0)
    ob = jnp.concatenate(attended, axis=0)
    hidden = in_f + active * mixed
    scale_two = lax.rsqrt(jnp.mean(hidden * hidden, axis=-1, keepdims=True) + EPSILON)
    hn2 = (hidden * scale_two * gain_two).astype(BF)
    hn2, hidden, scale_two, hn1_core, df_core = tie(hn2, hidden, scale_two, hn1_core, df_core)

    g = dot(hn2, w_gate)
    u = dot(hn2, w_up)
    sig = jax.nn.sigmoid(g)
    silu = g * sig
    z = (silu * u).astype(BF)
    dg = (dz * u * sig * (1.0 + g * (1.0 - sig))).astype(BF)
    du = (dz * silu).astype(BF)
    z, dg, du = tie(z, dg, du)

    z_other = to_chip(half(z, 1 - chip))
    dn2_part = (dot_t(dg, w_gate) + dot_t(du, w_up)).astype(BF)
    z_other, dn2_part, dg, du, hn2 = tie(z_other, dn2_part, dg, du, hn2)
    hn2_other = to_chip(hn2)

    dn2_other = swap_tensor(dn2_part)
    z_chip = by_chip(half(z, chip), z_other)
    dgu_other = to_chip(jnp.concatenate([half(dg, 1 - chip), half(du, 1 - chip)], axis=1))
    down_quarter, hidden = tie(dot_rows(z_chip, df_core), hidden)
    down_part = lax.psum_scatter(down_quarter, "seq", scatter_dimension=0, tiled=True)
    dn2 = dn2_part.astype(F32) + dn2_other
    grad_f = g_in.astype(F32)
    d_scaled = dn2 * gain_two
    inner_two = jnp.mean(d_scaled * hidden, axis=-1, keepdims=True)
    dh = grad_f + scale_two * d_scaled - hidden * scale_two**3 * inner_two
    gain_terms = mine(jnp.sum(dn2 * hidden * scale_two, axis=0))
    da = (active * dh).astype(BF)
    do = dot_t(da, w_out).astype(BF)
    da_other = to_chip(da)
    o_other = to_chip(half(ob, 1 - chip))
    dqs = []
    dkvs = []
    for m in range(micro):
        dq, dkv = attention(m, length, q, kv_all, query_pos, key_pos, do, cos, sin)
        dqs.append(dq)
        dkvs.append(dkv)
    dqb = jnp.concatenate(dqs, axis=0)
    dkvs, dqb, hn2_other, dgu_other, down_part = tie(
        jnp.stack(dkvs), dqb, hn2_other, dgu_other, down_part
    )
    dkv = lax.psum_scatter(dkvs, "seq", scatter_dimension=1, tiled=True)

    hn2_core = by_core(hn2, hn2_other)
    dgu = jnp.concatenate([half(dg, chip), half(du, chip)], axis=1)
    dgu_chip = by_chip(dgu, dgu_other)
    gate_up_quarter = dot_rows(hn2_core, dgu_chip)
    dkv, da_other, o_other, gate_up_quarter = tie(dkv, da_other, o_other, gate_up_quarter)
    gate_up_part = lax.psum_scatter(gate_up_quarter, "seq", scatter_dimension=0, tiled=True)
    dq_part = dot_t(dqb, query_weight)
    branch = scatter_tensor(dot(z, w_down))
    da_core = by_core(da, da_other)
    o_chip = by_chip(half(ob, chip), o_other)
    out_quarter = dot_rows(o_chip, da_core)
    output = (mine(hidden) + active * branch).astype(BF)

    dkb, dvb = turn_back(dkv.reshape(rows, -1), cos, sin)
    grads = (dqb, dkb, dvb)
    widths = tuple(a.shape[1] // 2 for a in grads)
    qkv_other = to_chip(jnp.concatenate([half(a, 1 - chip) for a in grads], axis=1))
    qkv_own = jnp.concatenate([half(a, chip) for a in grads], axis=1)
    qkv_other, qkv_own = tie(qkv_other, qkv_own)
    qkv_chip = by_chip(qkv_own, qkv_other)
    qkv_quarter = dot_rows(hn1_core, qkv_chip)
    out_quarter, qkv_quarter, gate_up_part = tie(out_quarter, qkv_quarter, gate_up_part)
    results = share(down_part, gate_up_part, out_quarter, qkv_quarter, widths)

    dn1 = scatter_tensor(dq_part + dot_t(dkb, key_weight) + dot_t(dvb, value_weight))
    d_scaled_one = dn1 * gain_one_s
    in_slice = mine(in_f)
    inner_own = jnp.sum(d_scaled_one * in_slice, axis=-1)
    gains = jnp.stack([jnp.sum(dn1 * in_slice * scale_one, axis=0), gain_terms])
    inner_one = (inner_own + swap_tensor(inner_own))[:, None]
    input_grad = (
        mine(dh) + scale_one * d_scaled_one - in_slice * scale_one**3 * (inner_one / width)
    )
    gains = gains + to_chip(gains)
    gains = gains + to_core(gains)
    gains = gains + lax.ppermute(gains, "seq", PAIRS)
    gains = gains + lax.ppermute(gains, "seq", [(0, 2), (2, 0), (1, 3), (3, 1)])

    return (
        output.reshape(micro, 1, length, slice_width),
        input_grad.reshape(micro, 1, length, slice_width),
        gains[0],
        results["query"],
        results["key"],
        results["value"],
        results["out"],
        gains[1],
        results["gate"],
        results["up"],
        results["down"],
    )


def solution(mesh):
    return jax.shard_map(
        on_device,
        mesh=mesh,
        in_specs=(
            P(None, "dp", "seq", None),
            P(None, "dp"),
            P(None, "dp", None),
            P(),
            P(None, "tensor"),
            P(None, "tensor"),
            P(None, "tensor"),
            P("tensor", None),
            P(),
            P(None, "tensor"),
            P(None, "tensor"),
            P("tensor", None),
            P(None, "dp", "seq", None),
        ),
        out_specs=(
            P(None, "dp", "seq", "tensor"),
            P(None, "dp", "seq", "tensor"),
            P("tensor"),
            P(None, "tensor"),
            P(None, "tensor"),
            P(None, "tensor"),
            P("tensor", None),
            P("tensor"),
            P(None, "tensor"),
            P(None, "tensor"),
            P("tensor", None),
        ),
        check_vma=False,
    )
```

```python
import functools

import jax
import jax.numpy as jnp
from jax import lax
from jax.experimental import pallas as pl
from jax.experimental.pallas import tpu as pltpu
from jax.sharding import PartitionSpec as P

HEAD_DIMENSION = 128
EPSILON = 1e-05
NEGATIVE = -1e30
BF = jnp.bfloat16
F32 = jnp.float32
ACROSS = [(0, 2), (2, 0), (1, 3), (3, 1)]
CORES = [(0, 1), (1, 0), (2, 3), (3, 2)]
PAIRS = [(0, 1), (1, 0), (2, 3), (3, 2)]


def dot(a, b):
    return jnp.dot(a, b, preferred_element_type=F32)


def dot_t(a, b):
    return lax.dot_general(a, b, (((1,), (1,)), ((), ())), preferred_element_type=F32)


def dot_rows(a, b):
    out = lax.dot_general(a, b, (((0,), (0,)), ((), ())), preferred_element_type=F32)
    return out.astype(BF)


def swap_tensor(sent):
    if lax.axis_size("tensor") == 2:
        return lax.ppermute(sent, "tensor", [(0, 1), (1, 0)]).astype(F32)
    return lax.psum(sent.astype(F32), "tensor") - sent.astype(F32)


def half(values, index):
    width = values.shape[1] // 2
    return lax.dynamic_slice_in_dim(values, index * width, width, 1)


def to_core(sent):
    return lax.ppermute(sent, "dp", CORES)


def to_chip(sent):
    return lax.ppermute(sent, "dp", ACROSS)


def tables(positions):
    half_width = HEAD_DIMENSION // 2
    frequency = jnp.exp(
        jnp.arange(half_width, dtype=F32) * (-2.0 / HEAD_DIMENSION) * jnp.log(10000.0)
    )
    phases = positions.astype(F32)[:, None] * frequency[None, :]
    cos, sin = jnp.cos(phases), jnp.sin(phases)
    return jnp.concatenate([cos, cos], axis=1), jnp.concatenate([-sin, sin], axis=1)


def turn(values, cos, sin):
    return values * cos + pltpu.roll(values, HEAD_DIMENSION // 2, 1) * sin


def key_value_kernel(
    x_ref, gain_ref, key_ref, value_ref, cos_ref, sin_ref, out_ref, normed_ref, scale_ref
):
    @pl.when(pl.program_id(0) == 0)
    def _():
        for start in range(0, x_ref.shape[0], 32):
            rows = slice(start, start + 32)
            raw = x_ref[rows, :].astype(F32)
            scale = lax.rsqrt(jnp.mean(raw * raw, axis=-1, keepdims=True) + EPSILON)
            scale_ref[rows, :] = scale
            normed_ref[rows, :] = (raw * scale * gain_ref[...]).astype(BF)

    x = normed_ref[...]
    keys = dot(x, key_ref[...])
    values = dot(x, value_ref[...]).astype(BF)
    for start in range(0, keys.shape[1], HEAD_DIMENSION):
        head = slice(start, start + HEAD_DIMENSION)
        turned = turn(keys[:, head], cos_ref[...], sin_ref[...])
        out_ref[:, 2 * start : 2 * start + HEAD_DIMENSION] = turned.astype(BF)
        out_ref[:, 2 * start + HEAD_DIMENSION : 2 * (start + HEAD_DIMENSION)] = values[:, head]


def keys_and_values(x, gain, key_weight, value_weight, cos, sin):
    rows, width = x.shape
    columns = key_weight.shape[1]
    block = 2 * HEAD_DIMENSION if columns % (2 * HEAD_DIMENSION) == 0 else HEAD_DIMENSION
    whole = lambda step: (0, 0)
    column = lambda step: (0, step)
    return pl.pallas_call(
        key_value_kernel,
        grid=(columns // block,),
        in_specs=[
            pl.BlockSpec((rows, width), whole),
            pl.BlockSpec((1, width), whole),
            pl.BlockSpec((width, block), column),
            pl.BlockSpec((width, block), column),
            pl.BlockSpec((rows, HEAD_DIMENSION), whole),
            pl.BlockSpec((rows, HEAD_DIMENSION), whole),
        ],
        out_specs=[
            pl.BlockSpec((rows, 2 * block), column),
            pl.BlockSpec((rows, width), whole),
            pl.BlockSpec((rows, 1), whole),
        ],
        out_shape=[
            jax.ShapeDtypeStruct((rows, 2 * columns), BF),
            jax.ShapeDtypeStruct((rows, width), BF),
            jax.ShapeDtypeStruct((rows, 1), F32),
        ],
        name="keys_and_values",
    )(x, gain, key_weight, value_weight, cos, sin)


def query_kernel(x_ref, weight_ref, cos_ref, sin_ref, out_ref):
    raw = dot(x_ref[...], weight_ref[...])
    for start in range(0, raw.shape[1], HEAD_DIMENSION):
        head = raw[:, start : start + HEAD_DIMENSION]
        turned = turn(head, cos_ref[...], sin_ref[...])
        out_ref[:, start : start + HEAD_DIMENSION] = turned.astype(BF)


def queries(x, weight, cos, sin):
    rows, width = x.shape
    block = 2 * HEAD_DIMENSION
    whole = lambda step: (0, 0)
    column = lambda step: (0, step)
    return pl.pallas_call(
        query_kernel,
        grid=(weight.shape[1] // block,),
        in_specs=[
            pl.BlockSpec((rows, width), whole),
            pl.BlockSpec((width, block), column),
            pl.BlockSpec((rows, HEAD_DIMENSION), whole),
            pl.BlockSpec((rows, HEAD_DIMENSION), whole),
        ],
        out_specs=pl.BlockSpec((rows, block), column),
        out_shape=jax.ShapeDtypeStruct((rows, weight.shape[1]), BF),
        cost_estimate=pl.CostEstimate(
            flops=2 * rows * width * weight.shape[1],
            bytes_accessed=2 * width * weight.shape[1] + 2 * rows * width,
            transcendentals=0,
        ),
        name="queries",
    )(x, weight, cos, sin)


def probabilities(query, keys, query_pos, key_pos):
    scores = dot_t(query, keys) * HEAD_DIMENSION ** (-0.5)
    scores = jnp.where(key_pos <= query_pos, scores, NEGATIVE)
    expd = jnp.exp(scores - jnp.max(scores, axis=-1, keepdims=True))
    return expd / jnp.sum(expd, axis=-1, keepdims=True)


def attend_kernel(q_ref, kv_ref, query_pos_ref, key_pos_ref, out_ref):
    keys = kv_ref[:, :HEAD_DIMENSION]
    values = kv_ref[:, HEAD_DIMENSION:]
    for start in range(0, q_ref.shape[1], HEAD_DIMENSION):
        head = slice(start, start + HEAD_DIMENSION)
        prob = probabilities(q_ref[:, head], keys, query_pos_ref[...], key_pos_ref[...])
        out_ref[:, head] = dot(prob.astype(BF), values).astype(BF)


def attend_back_kernel(
    q_ref, kv_ref, query_pos_ref, key_pos_ref, do_ref, cos_ref, sin_ref, dq_ref, dkv_ref
):
    keys = kv_ref[:, :HEAD_DIMENSION]
    values = kv_ref[:, HEAD_DIMENSION:]
    dk = dv = None
    for start in range(0, q_ref.shape[1], HEAD_DIMENSION):
        head = slice(start, start + HEAD_DIMENSION)
        query = q_ref[:, head]
        do = do_ref[:, head]
        prob = probabilities(query, keys, query_pos_ref[...], key_pos_ref[...])
        dp = dot_t(do, values)
        inner = jnp.sum(prob * dp, axis=-1, keepdims=True)
        ds = (prob * (dp - inner) * HEAD_DIMENSION ** (-0.5)).astype(BF)
        dq = dot(ds, keys)
        dq_ref[:, head] = turn(dq, cos_ref[...], -sin_ref[...]).astype(BF)
        part_k = lax.dot_general(ds, query, (((0,), (0,)), ((), ())), preferred_element_type=F32)
        part_v = lax.dot_general(
            prob.astype(BF), do, (((0,), (0,)), ((), ())), preferred_element_type=F32
        )
        dk = part_k if dk is None else dk + part_k
        dv = part_v if dv is None else dv + part_v
    dkv_ref[:, :HEAD_DIMENSION] = dk.astype(BF)
    dkv_ref[:, HEAD_DIMENSION:] = dv.astype(BF)


def attention(m, length, q, kv_all, query_pos, key_pos, do=None, cos=None, sin=None):
    _, total, both = kv_all.shape
    heads = both // (2 * HEAD_DIMENSION)
    block = q.shape[1] // heads
    in_rows = lambda h: (m, h)
    column = lambda h: (0, h)
    in_specs = [
        pl.BlockSpec((length, block), in_rows),
        pl.BlockSpec((None, total, 2 * HEAD_DIMENSION), lambda h: (m, 0, h)),
        pl.BlockSpec((length, 1), lambda h: (m, 0)),
        pl.BlockSpec((None, 1, total), lambda h: (m, 0, 0)),
    ]
    operands = [q, kv_all, query_pos, key_pos]
    out_specs = pl.BlockSpec((length, block), column)
    out_shape = jax.ShapeDtypeStruct((length, q.shape[1]), BF)
    kernel = attend_kernel
    if do is not None:
        kernel = attend_back_kernel
        in_specs += [pl.BlockSpec((length, block), in_rows)]
        in_specs += [pl.BlockSpec((length, HEAD_DIMENSION), lambda h: (m, 0))] * 2
        operands += [do, cos, sin]
        out_specs = [out_specs, pl.BlockSpec((total, 2 * HEAD_DIMENSION), column)]
        out_shape = [out_shape, jax.ShapeDtypeStruct((total, both), BF)]
    return pl.pallas_call(
        kernel,
        grid=(heads,),
        in_specs=in_specs,
        out_specs=out_specs,
        out_shape=out_shape,
        cost_estimate=pl.CostEstimate(
            flops=(4 if do is None else 10) * length * total * q.shape[1],
            bytes_accessed=8 * total * both,
            transcendentals=length * total * q.shape[1] // HEAD_DIMENSION,
        ),
        name="attend" if do is None else "attend_back",
    )(*operands)


def turn_back_kernel(dkv_ref, cos_ref, sin_ref, dk_ref, dv_ref):
    dk = dkv_ref[:, :HEAD_DIMENSION].astype(F32)
    dk_ref[...] = turn(dk, cos_ref[...], -sin_ref[...]).astype(BF)
    dv_ref[...] = dkv_ref[:, HEAD_DIMENSION:]


def turn_back(dkv, cos, sin):
    rows, both = dkv.shape
    column = lambda h: (0, h)
    return pl.pallas_call(
        turn_back_kernel,
        grid=(both // (2 * HEAD_DIMENSION),),
        in_specs=[pl.BlockSpec((rows, 2 * HEAD_DIMENSION), column)]
        + [pl.BlockSpec((rows, HEAD_DIMENSION), lambda h: (0, 0))] * 2,
        out_specs=[pl.BlockSpec((rows, HEAD_DIMENSION), column)] * 2,
        out_shape=[jax.ShapeDtypeStruct((rows, both // 2), BF)] * 2,
        name="turn_back",
    )(dkv, cos, sin)


def share_kernel(every_ref, *out_refs, pieces):
    out_refs = list(out_refs)
    for start, stop, widths in pieces:
        size = stop - start
        at = 0
        for width in widths:
            out_ref = out_refs.pop(0)
            for i in range(every_ref.shape[0]):
                source = every_ref[i, start:stop, at : at + width]
                out_ref[i * size : (i + 1) * size, :] = source.astype(F32)
            at += width


def write_whole(every, pieces):
    count, rows, cols = every.shape
    seq = lax.axis_size("seq")
    aligned = all(size % 16 == 0 and all(w % 128 == 0 for w in ws) for size, ws, _ in pieces)
    if not aligned:
        results = []
        start = 0
        for size, widths, row_by_core in pieces:
            at = 0
            for width in widths:
                piece = every[:, start : start + size, at : at + width]
                piece = piece.reshape(seq, 2, 2, size, width)
                piece = piece.transpose((2, 0, 3, 1, 4) if row_by_core else (1, 0, 3, 2, 4))
                results.append(piece.reshape(2 * seq * size, 2 * width).astype(F32))
                at += width
            start += size
        return results
    spans = []
    out_specs = []
    out_shape = []
    start = 0
    for size, widths, row_by_core in pieces:
        spans.append((start, start + size, widths))

        def index(device, row_by_core=row_by_core):
            chip, core = device // 2, device % 2
            return (core, chip) if row_by_core else (chip, core)

        for width in widths:
            out_specs.append(pl.BlockSpec((seq * size, width), index))
            out_shape.append(jax.ShapeDtypeStruct((2 * seq * size, 2 * width), F32))
        start += size
    return pl.pallas_call(
        functools.partial(share_kernel, pieces=tuple(spans)),
        grid=(count // seq,),
        in_specs=[pl.BlockSpec((seq, None, rows, cols), lambda device: (0, device, 0, 0))],
        out_specs=out_specs,
        out_shape=out_shape,
        cost_estimate=pl.CostEstimate(
            flops=0, bytes_accessed=6 * every.size, transcendentals=0
        ),
        compiler_params=pltpu.CompilerParams(vmem_limit_bytes=48 * 2**20),
        name="write_whole",
    )(every.reshape(seq, count // seq, rows, cols))


def share(down_part, gate_up_part, out_quarter, qkv_quarter, widths):
    half_ff = gate_up_part.shape[1] // 2
    gate_up = lax.all_gather(gate_up_part, ("seq", "dp"), axis=0, tiled=False)
    gate, up = write_whole(gate_up, [(gate_up_part.shape[0], (half_ff, half_ff), True)])
    seq = lax.axis_size("seq")
    cols = out_quarter.shape[1]
    out_rows, qkv_rows = out_quarter.shape[0] // seq, qkv_quarter.shape[0] // seq
    down_rows = down_part.shape[0]
    if qkv_quarter.shape[1] == cols:
        joined = jnp.concatenate(
            [out_quarter.reshape(seq, out_rows, cols), qkv_quarter.reshape(seq, qkv_rows, cols)],
            axis=1,
        )
        part = lax.psum_scatter(joined, "seq", scatter_dimension=0, tiled=False)
        part = jnp.concatenate([down_part, part.reshape(out_rows + qkv_rows, cols)], axis=0)
        every = lax.all_gather(part, ("seq", "dp"), axis=0, tiled=False)
        down, out, query, key, value = write_whole(
            every,
            [(down_rows, (cols,), False), (out_rows, (cols,), False), (qkv_rows, widths, True)],
        )
    else:
        out_part = lax.psum_scatter(out_quarter, "seq", scatter_dimension=0, tiled=True)
        qkv_part = lax.psum_scatter(qkv_quarter, "seq", scatter_dimension=0, tiled=True)
        part = jnp.concatenate([down_part, out_part], axis=0)
        every = lax.all_gather(part, ("seq", "dp"), axis=0, tiled=False)
        down, out = write_whole(
            every, [(down_rows, (cols,), False), (out_rows, (cols,), False)]
        )
        every = lax.all_gather(qkv_part, ("seq", "dp"), axis=0, tiled=False)
        query, key, value = write_whole(every, [(qkv_rows, widths, True)])
    return dict(gate=gate, up=up, down=down, out=out, query=query, key=key, value=value)


def tie(*values):
    return lax.optimization_barrier(values)


def on_device(
    inputs,
    skip_mask,
    block_order,
    norm1_gain,
    query_weight,
    key_weight,
    value_weight,
    w_out,
    norm2_gain,
    w_gate,
    w_up,
    w_down,
    out_grad,
):
    tensor_count = lax.axis_size("tensor")
    tensor_rank = lax.axis_index("tensor")
    seq_rank = lax.axis_index("seq")
    me = lax.axis_index("dp")
    chip, core = me // 2, me % 2
    micro, _, length, width = inputs.shape
    rows = micro * length
    slice_width = width // tensor_count
    core_half = width // 2
    block_rows = length // 2
    col_start = tensor_rank * slice_width

    def mine(values):
        return lax.dynamic_slice_in_dim(values, col_start, slice_width, values.ndim - 1)

    def scatter_tensor(part):
        if tensor_count != 2:
            sent = part.astype(BF)
            got = lax.psum_scatter(sent, "tensor", scatter_dimension=1, tiled=True)
            return got.astype(F32)
        sent = lax.dynamic_slice_in_dim(
            part, (1 - tensor_rank) * slice_width, slice_width, 1
        ).astype(BF)
        return mine(part) + swap_tensor(sent)

    gain_one = norm1_gain.astype(F32)
    gain_two = norm2_gain.astype(F32)
    gain_one_s = mine(gain_one)

    x_in = inputs.reshape(rows, width)
    g_in = out_grad.reshape(rows, width)
    in_f = x_in.astype(F32)
    offsets = jnp.arange(block_rows, dtype=jnp.int32)
    order = block_order[:, 0]
    key_pos = (order[:, :, None] * block_rows + offsets).reshape(micro, 1, -1)
    my_blocks = lax.dynamic_slice_in_dim(order, 2 * seq_rank, 2, 1)
    query_pos = (my_blocks[:, :, None] * block_rows + offsets).reshape(rows, 1)
    cos, sin = tables(query_pos[:, 0])

    kvb, hn1, scale_one = keys_and_values(
        x_in, gain_one[None], key_weight, value_weight, cos, sin
    )
    kvb, hn1, g_in, skips = tie(kvb, hn1, g_in, skip_mask[:, 0])
    active = jnp.repeat((1 - skips).astype(F32), length)[:, None]
    df = (active * g_in.astype(F32)).astype(BF)

    kv_all = lax.all_gather(kvb.reshape(micro, length, -1), "seq", axis=1, tiled=True)
    hn1_other = to_chip(hn1)
    df_other = to_chip(df)
    q = queries(hn1, query_weight, cos, sin)
    dz = dot_t(df, w_down)
    kv_all, q, dz = tie(kv_all, q, dz)

    def by_core(own, other):
        both = jnp.concatenate([own, other], axis=0)
        return jnp.concatenate([half(both, core), to_core(half(both, 1 - core))], axis=0)

    def by_chip(own, other):
        both = jnp.concatenate([own, other], axis=0)
        return jnp.concatenate([both, to_core(both)], axis=0)

    attended = []
    parts = []
    others = []
    for m in range(micro):
        o = attention(m, length, q, kv_all, query_pos, key_pos)
        attended.append(o)
        part = dot(o, w_out).astype(BF)
        parts.append(part)
        others.append(swap_tensor(part))
    hn1_other, df_other, attended[-1] = tie(hn1_other, df_other, attended[-1])
    hn1_core = by_core(hn1, hn1_other)
    df_core = by_core(df, df_other)
    mixed = jnp.concatenate([a.astype(F32) + b for a, b in zip(parts, others)], axis=0)
    ob = jnp.concatenate(attended, axis=0)
    hidden = in_f + active * mixed
    scale_two = lax.rsqrt(jnp.mean(hidden * hidden, axis=-1, keepdims=True) + EPSILON)
    hn2 = (hidden * scale_two * gain_two).astype(BF)
    hn2, hidden, scale_two, hn1_core, df_core = tie(hn2, hidden, scale_two, hn1_core, df_core)

    g = dot(hn2, w_gate)
    u = dot(hn2, w_up)
    sig = jax.nn.sigmoid(g)
    silu = g * sig
    z = (silu * u).astype(BF)
    dg = (dz * u * sig * (1.0 + g * (1.0 - sig))).astype(BF)
    du = (dz * silu).astype(BF)
    z, dg, du = tie(z, dg, du)

    z_other = to_chip(half(z, 1 - chip))
    dn2_part = (dot_t(dg, w_gate) + dot_t(du, w_up)).astype(BF)
    z_other, dn2_part, dg, du, hn2 = tie(z_other, dn2_part, dg, du, hn2)
    hn2_other = to_chip(hn2)

    dn2_other = swap_tensor(dn2_part)
    z_chip = by_chip(half(z, chip), z_other)
    dgu_other = to_chip(jnp.concatenate([half(dg, 1 - chip), half(du, 1 - chip)], axis=1))
    down_quarter, hidden = tie(dot_rows(z_chip, df_core), hidden)
    down_part = lax.psum_scatter(down_quarter, "seq", scatter_dimension=0, tiled=True)
    dn2 = dn2_part.astype(F32) + dn2_other
    grad_f = g_in.astype(F32)
    d_scaled = dn2 * gain_two
    inner_two = jnp.mean(d_scaled * hidden, axis=-1, keepdims=True)
    dh = grad_f + scale_two * d_scaled - hidden * scale_two**3 * inner_two
    gain_terms = mine(jnp.sum(dn2 * hidden * scale_two, axis=0))
    da = (active * dh).astype(BF)
    do = dot_t(da, w_out).astype(BF)
    da_other = to_chip(da)
    o_other = to_chip(half(ob, 1 - chip))
    dqs = []
    dkvs = []
    for m in range(micro):
        dq, dkv = attention(m, length, q, kv_all, query_pos, key_pos, do, cos, sin)
        dqs.append(dq)
        dkvs.append(dkv)
    dqb = jnp.concatenate(dqs, axis=0)
    dkvs, dqb, hn2_other, dgu_other, down_part = tie(
        jnp.stack(dkvs), dqb, hn2_other, dgu_other, down_part
    )
    dkv = lax.psum_scatter(dkvs, "seq", scatter_dimension=1, tiled=True)

    hn2_core = by_core(hn2, hn2_other)
    dgu = jnp.concatenate([half(dg, chip), half(du, chip)], axis=1)
    dgu_chip = by_chip(dgu, dgu_other)
    gate_up_quarter = dot_rows(hn2_core, dgu_chip)
    dkv, da_other, o_other, gate_up_quarter = tie(dkv, da_other, o_other, gate_up_quarter)
    gate_up_part = lax.psum_scatter(gate_up_quarter, "seq", scatter_dimension=0, tiled=True)
    dq_part = dot_t(dqb, query_weight)
    branch = scatter_tensor(dot(z, w_down))
    da_core = by_core(da, da_other)
    o_chip = by_chip(half(ob, chip), o_other)
    out_quarter = dot_rows(o_chip, da_core)
    output = (mine(hidden) + active * branch).astype(BF)

    dkb, dvb = turn_back(dkv.reshape(rows, -1), cos, sin)
    grads = (dqb, dkb, dvb)
    widths = tuple(a.shape[1] // 2 for a in grads)
    qkv_other = to_chip(jnp.concatenate([half(a, 1 - chip) for a in grads], axis=1))
    qkv_own = jnp.concatenate([half(a, chip) for a in grads], axis=1)
    qkv_other, qkv_own = tie(qkv_other, qkv_own)
    qkv_chip = by_chip(qkv_own, qkv_other)
    qkv_quarter = dot_rows(hn1_core, qkv_chip)
    out_quarter, qkv_quarter, gate_up_part = tie(out_quarter, qkv_quarter, gate_up_part)
    results = share(down_part, gate_up_part, out_quarter, qkv_quarter, widths)

    dn1 = scatter_tensor(dq_part + dot_t(dkb, key_weight) + dot_t(dvb, value_weight))
    d_scaled_one = dn1 * gain_one_s
    in_slice = mine(in_f)
    inner_own = jnp.sum(d_scaled_one * in_slice, axis=-1)
    gains = jnp.stack([jnp.sum(dn1 * in_slice * scale_one, axis=0), gain_terms])
    inner_one = (inner_own + swap_tensor(inner_own))[:, None]
    input_grad = (
        mine(dh) + scale_one * d_scaled_one - in_slice * scale_one**3 * (inner_one / width)
    )
    gains = gains + to_chip(gains)
    gains = gains + to_core(gains)
    gains = gains + lax.ppermute(gains, "seq", PAIRS)
    gains = gains + lax.ppermute(gains, "seq", [(0, 2), (2, 0), (1, 3), (3, 1)])

    return (
        output.reshape(micro, 1, length, slice_width),
        input_grad.reshape(micro, 1, length, slice_width),
        gains[0],
        results["query"],
        results["key"],
        results["value"],
        results["out"],
        gains[1],
        results["gate"],
        results["up"],
        results["down"],
    )


def solution(mesh):
    return jax.shard_map(
        on_device,
        mesh=mesh,
        in_specs=(
            P(None, "dp", "seq", None),
            P(None, "dp"),
            P(None, "dp", None),
            P(),
            P(None, "tensor"),
            P(None, "tensor"),
            P(None, "tensor"),
            P("tensor", None),
            P(),
            P(None, "tensor"),
            P(None, "tensor"),
            P("tensor", None),
            P(None, "dp", "seq", None),
        ),
        out_specs=(
            P(None, "dp", "seq", "tensor"),
            P(None, "dp", "seq", "tensor"),
            P("tensor"),
            P(None, "tensor"),
            P(None, "tensor"),
            P(None, "tensor"),
            P("tensor", None),
            P("tensor"),
            P(None, "tensor"),
            P(None, "tensor"),
            P("tensor", None),
        ),
        check_vma=False,
    )
```
